128 devices in a mesh: ifg: 32 (over y, x, z_hi), row: 4 (over z_lo, core).
Axes of the slice: x: 4, y: 4, z: 4 (z_hi: 2, z_lo: 2; z = z_hi * 2 + z_lo), core: 2. Of those that a mesh axis runs over, the one named last changes fastest.
Arguments:
- ifg_real: bfloat16 [1024, 256, 512], P('ifg', 'row'), may hold values from -6 to 6
- ifg_imag: bfloat16 [1024, 256, 512], P('ifg', 'row'), may hold values from -6 to 6
- date_pairs: int32 [1024, 2], replicated, may hold values from 0 to 319, as said below
Outputs:
- corrected: float32 [320, 256, 512], P('ifg', 'row')
- atmosphere: float32 [320, 256, 512], P('ifg', 'row')
The draws below stay inside these ranges and needn't reach their ends.
Inputs may be any that keep to these rules, and one draw needn't show every extreme that they name: `date_pairs`: each row holds a reference date and a later secondary date, 1 to 5 dates apart.
All inputs are finite; a program needn't handle non-finite values.
Results may differ from the reference program's by a relative error of at most 0.0078.
Values may be sent and summed in bfloat16 or wider, within the bound.
No kernel may reach another device: no remote copies, remote signals or barrier semaphores. Data moves between devices by JAX's collectives and lax.ppermute only.
A program may use at most 128 MiB of HBM per device.

```python
import math
import jax
import jax.numpy as jnp
from jax import lax

COLS = 512
PATCH = 64
NDATES = 320
ITERS = 3
RADIUS = 16
NIFG = 1024
ROWS = 256


def draw_date_pairs(key, part):
    key_spacing = jax.random.fold_in(key, 11)
    key_earlier = jax.random.fold_in(key, 12)
    spacing = jax.random.randint(key_spacing, (NIFG,), 1, 6)
    earlier = jax.random.randint(key_earlier, (NIFG,), 0, NDATES - 5)
    position = jnp.arange(NIFG)
    earlier = jnp.where(position == 0, 0, earlier)
    earlier = jnp.where(position == NIFG - 1, NDATES - 1 - spacing, earlier)
    return jnp.stack([earlier, earlier + spacing], axis=1).astype(jnp.int32)


def block_levels(key, shape, cuts, least, top_value):
    factor_of, own = 1.0, jax.random.fold_in(key, 6)
    for dim, blocks in cuts:
        steps = jnp.exp(jax.random.uniform(jax.random.fold_in(own, dim), (blocks,), jnp.float32, least / len(cuts), top_value / len(cuts)))
        factor_of = factor_of * jnp.repeat(steps, shape[dim] // blocks).reshape([-1 if axis == dim else 1 for axis in range(len(shape))])
    return factor_of


def noise(own_key, dims, spread, limit, cuts=(), kind=jnp.bfloat16):
    gain = block_levels(own_key, dims, cuts, -0.22, 0.18) if cuts else 1.0
    array = jax.random.normal(own_key, dims, jnp.float32) * spread * gain
    return jnp.minimum(jnp.maximum(array, -limit), limit).astype(kind)


def setup_inputs(seed: int = 0) -> dict:
    splits = jax.random.split(jax.random.key(seed), 4)
    ifg_real = noise(splits[0], (NIFG, ROWS, COLS), 1.0, 6.0, ((0, 32), (1, 4)))
    ifg_imag = noise(splits[1], (NIFG, ROWS, COLS), 1.0, 6.0, ((0, 32), (1, 4)))
    date_pairs = draw_date_pairs(jax.random.fold_in(splits[3], 71), 0)
    return dict(ifg_real=ifg_real, ifg_imag=ifg_imag, date_pairs=date_pairs)


goldstein_power = 0.5
huber_threshold = 0.3
blur_sigma = 5.0
ridge_weight = 1.0

def spectral_tables():
    counter = jnp.arange(PATCH, dtype=jnp.int32)
    phase_steps = counter[:, None] * counter[None, :] % PATCH
    angles = phase_steps.astype(jnp.float32) * (2.0 * math.pi / PATCH)
    scaling = 1.0 / math.sqrt(PATCH)
    cosine = jnp.cos(angles) * scaling
    sine_lookup = jnp.sin(angles) * scaling
    forward = jnp.concatenate([jnp.concatenate([cosine, -sine_lookup], 1), jnp.concatenate([sine_lookup, cosine], 1)], 0)
    inverse = jnp.concatenate([jnp.concatenate([cosine, sine_lookup], 1), jnp.concatenate([-sine_lookup, cosine], 1)], 0)
    taper_row = jnp.sin(math.pi * (jnp.arange(PATCH, dtype=jnp.float32) + 0.5) / PATCH) ** 2
    return (forward.astype(jnp.bfloat16), inverse.astype(jnp.bfloat16), cosine.astype(jnp.bfloat16), sine_lookup.astype(jnp.bfloat16), taper_row)

def row_apply(values, cosine, sine_lookup, direction):
    flipped = jnp.concatenate([values[..., PATCH:], -values[..., :PATCH]], axis=-1)
    first = jnp.einsum('kb,anbcl->ankcl', cosine.astype(jnp.float32), values.astype(jnp.float32))
    second = jnp.einsum('kb,anbcl->ankcl', sine_lookup.astype(jnp.float32), flipped.astype(jnp.float32))
    return first + direction * second

def filter_block(padded, tables):
    forward, inverse, cosine, sine_lookup, taper_row = tables
    block_count = padded.shape[0]
    rows_pad = padded.shape[2]
    cols_pad = padded.shape[3]
    half_patch = PATCH // 2
    taper_both = jnp.concatenate([taper_row, taper_row])
    canvas = jnp.zeros((block_count, 2, rows_pad, cols_pad), jnp.float32)
    for row_shift in (0, half_patch):
        for col_shift in (0, half_patch):
            window = padded[:, :, row_shift:rows_pad - row_shift, col_shift:cols_pad - col_shift]
            row_tiles = window.shape[2] // PATCH
            col_tiles = window.shape[3] // PATCH
            tile_grid = window.reshape(block_count, 2, row_tiles, PATCH, col_tiles, PATCH)
            stacked = jnp.concatenate([tile_grid[:, 0], tile_grid[:, 1]], axis=-1)
            column_spectra = jnp.einsum('anbcl,lm->anbcm', stacked.astype(jnp.float32), forward.astype(jnp.float32)).astype(jnp.bfloat16)
            spectra = row_apply(column_spectra, cosine, sine_lookup, 1.0)
            spectral_power = spectra[..., :PATCH] ** 2 + spectra[..., PATCH:] ** 2 + 1.0
            shaping = spectral_power ** (0.5 * goldstein_power)
            shaped = (spectra * jnp.concatenate([shaping, shaping], axis=-1)).astype(jnp.bfloat16)
            row_back = row_apply(shaped, cosine, sine_lookup, -1.0).astype(jnp.bfloat16)
            restored = jnp.einsum('anbcl,lm->anbcm', row_back.astype(jnp.float32), inverse.astype(jnp.float32))
            weighted = restored * taper_row[:, None, None] * taper_both
            pieces = jnp.stack([weighted[..., :PATCH], weighted[..., PATCH:]], axis=1)
            pieces = pieces.reshape(block_count, 2, row_tiles * PATCH, col_tiles * PATCH)
            canvas = canvas + jnp.pad(pieces, ((0, 0), (0, 0), (row_shift, row_shift), (col_shift, col_shift)))
    return canvas[:, :, half_patch:rows_pad - half_patch, half_patch:cols_pad - half_patch]

def sine_of(real_part, imag_part):
    real_wide = real_part.astype(jnp.float32)
    imag_wide = imag_part.astype(jnp.float32)
    return (imag_wide / jnp.sqrt(real_wide * real_wide + imag_wide * imag_wide + 1.0)).astype(jnp.bfloat16)

def projection(date_pairs):
    date_index = jnp.arange(NDATES, dtype=jnp.int32)
    design = (date_pairs[:, 1:2] == date_index[None, :]).astype(jnp.float32) - (date_pairs[:, 0:1] == date_index[None, :]).astype(jnp.float32)
    gram = jnp.dot(design.T, design, precision=lax.Precision.HIGHEST) + ridge_weight * jnp.eye(NDATES, dtype=jnp.float32)
    cholesky_factor = jnp.linalg.cholesky(gram)
    halfway = lax.linalg.triangular_solve(cholesky_factor, design.T, left_side=True, lower=True)
    mapping = lax.linalg.triangular_solve(cholesky_factor, halfway, left_side=True, lower=True, transpose_a=True)
    return (design, mapping)

def invert(observed_sines, design, mapping):
    observed = observed_sines.astype(jnp.float32)
    series = jnp.zeros((NDATES, observed.shape[1]), jnp.float32)
    misfit = observed
    for iteration in range(ITERS):
        if iteration > 0:
            misfit = observed - jnp.dot(design, series, precision=lax.Precision.HIGHEST)
        series = series + jnp.dot(mapping, jnp.clip(misfit, -huber_threshold, huber_threshold), precision=lax.Precision.HIGHEST)
    return series

def gauss_matrix(size_out, size_in, offset):
    out_index = jnp.arange(size_out, dtype=jnp.int32)[:, None]
    in_index = jnp.arange(size_in, dtype=jnp.int32)[None, :]
    distance = in_index - offset - out_index
    kernel = jnp.exp(-0.5 * (distance.astype(jnp.float32) / blur_sigma) ** 2)
    return jnp.where(jnp.abs(distance) <= RADIUS, kernel, 0.0)

def reference(ifg_real, ifg_imag, date_pairs):
    tables = spectral_tables()
    half_patch = PATCH // 2
    joined = jnp.stack([ifg_real, ifg_imag], axis=1)
    padded = jnp.pad(joined, ((0, 0), (0, 0), (half_patch, half_patch), (half_patch, half_patch)))
    block_list = padded.reshape(NIFG // 2, 2, 2, ROWS + PATCH, COLS + PATCH)

    def run_block(block_data):
        return filter_block(block_data, tables).astype(jnp.bfloat16)
    filtered = lax.map(run_block, block_list).reshape(NIFG, 2, ROWS, COLS)
    phase_sines = sine_of(filtered[:, 0], filtered[:, 1])
    design, mapping = projection(date_pairs)
    series = invert(phase_sines.reshape(NIFG, ROWS * COLS), design, mapping).reshape(NDATES, ROWS, COLS)
    col_kernel = gauss_matrix(COLS, COLS, 0)
    row_filter_kernel = gauss_matrix(ROWS, ROWS, 0)
    smoothed_columns = jnp.einsum('drc,ce->dre', series, col_kernel, precision=lax.Precision.HIGHEST)
    smoothed_phase = jnp.einsum('om,nmb->nob', row_filter_kernel, smoothed_columns, precision=lax.Precision.HIGHEST)
    weight = lax.optimization_barrier(jnp.sum(row_filter_kernel, axis=1))[:, None] * lax.optimization_barrier(jnp.sum(col_kernel, axis=0))[None, :]
    atmosphere = smoothed_phase / weight
    return (series - atmosphere, atmosphere)
```

```python
import math

import jax
import jax.numpy as jnp
import ml_dtypes
import numpy as np
from jax import lax
from jax.experimental import pallas as pl
from jax.experimental.pallas import tpu as pltpu
from jax.sharding import PartitionSpec as P

PATCH = 64
HALF = PATCH // 2
NDATES = 320
ITERS = 3
RADIUS = 16
SIGMA = 5.0
THRESHOLD = 0.3
BAND = 5
LANES = 128
DATE_PAD = 384
BF16 = jnp.bfloat16
F32 = jnp.float32


def bf16(x):
    return np.asarray(x, np.float32).astype(ml_dtypes.bfloat16)


def tables():
    n = np.arange(PATCH)
    angle = (n[:, None] * n[None, :] % PATCH) * (2.0 * math.pi / PATCH)
    c = bf16(np.cos(angle) / 8.0).astype(np.float64)
    s = bf16(np.sin(angle) / 8.0).astype(np.float64)
    taper = np.sin(math.pi * (n + 0.5) / PATCH) ** 2
    two = np.eye(2)
    zero = np.zeros((PATCH, PATCH))

    rows_centre = np.block([[c, s], [-s, c]])
    up = np.concatenate([np.eye(PATCH), zero], 1)
    low = np.concatenate([zero, np.eye(PATCH)], 1)
    rows_edge = np.block(
        [[c @ up, s @ up], [c @ low, s @ low], [-s @ up, c @ up], [-s @ low, c @ low]]
    )
    c2, s2 = np.kron(two, c), np.kron(two, s)
    cols = np.block([[c2, -s2], [s2, c2]])
    shift = np.zeros((2, LANES, LANES))
    for i in range(LANES):
        if i < HALF:
            shift[0, LANES - HALF + i, i] = 1.0
        else:
            shift[1, i - HALF, i] = 1.0
    left, right = np.kron(two, shift[0]), np.kron(two, shift[1])
    t2 = np.concatenate([taper, taper])
    inv = np.block([[c2 * t2, s2 * t2], [-s2 * t2, c2 * t2]])
    forward = np.stack([cols, left @ cols, right @ cols])
    inverse = np.stack([inv, inv @ left.T, inv @ right.T])
    ct, st = c * taper[:, None], s * taper[:, None]
    top = np.concatenate([ct[HALF:], np.zeros((HALF, PATCH))], 0)
    top_s = np.concatenate([st[HALF:], np.zeros((HALF, PATCH))], 0)
    bot = np.concatenate([np.zeros((HALF, PATCH)), ct[:HALF]], 0)
    bot_s = np.concatenate([np.zeros((HALF, PATCH)), st[:HALF]], 0)
    back_centre = np.block([[ct, -st], [st, ct]])
    back_edge = np.block([[top, bot, -top_s, -bot_s], [top_s, bot_s, top, bot]])
    return tuple(
        bf16(x) for x in (rows_centre, rows_edge, forward, inverse, back_centre, back_edge)
    )


def gauss(distance):
    return np.where(np.abs(distance) <= RADIUS, np.exp(-0.5 * (distance / SIGMA) ** 2), 0.0)


def blur_tables(rows, local_rows, cols):
    i = np.arange(cols)
    by_col = gauss(i[:, None] - i[None, :])
    by_col = by_col / by_col.sum(0, keepdims=True)
    out = np.arange(rows)[:, None]
    src = np.arange(-RADIUS, rows + RADIUS)[None, :]
    by_row = gauss(src - out) * ((src >= 0) & (src < rows))
    by_row = by_row / by_row.sum(1, keepdims=True)
    blocks = [
        by_row[a : a + local_rows, a : a + local_rows + 2 * RADIUS]
        for a in range(0, rows, local_rows)
    ]
    return by_col.astype(np.float32), np.stack(blocks).astype(np.float32)


def mm(a, b):
    return jnp.dot(a, b, preferred_element_type=F32)


def spectral(y_re, y_im, fwd, inv):
    count = y_re.shape[1] // LANES
    pieces = []
    for c in range(count):
        sl = slice(c * LANES, (c + 1) * LANES)
        pieces.append(jnp.concatenate([y_re[:, sl], y_im[:, sl]], axis=1))
    f0, f_left, f_right = fwd[0], fwd[1], fwd[2]
    g0, g_left, g_right = inv[0], inv[1], inv[2]

    def shaped(z):
        re, im = z[:, :LANES], z[:, LANES:]
        scale = lax.rsqrt(lax.rsqrt(re * re + im * im + 1.0))
        return jnp.concatenate([(re * scale).astype(BF16), (im * scale).astype(BF16)], axis=1)

    even = []
    for c in range(count + 1):
        z = None
        if c > 0:
            z = mm(pieces[c - 1], f_left)
        if c < count:
            w = mm(pieces[c], f_right)
            z = w if z is None else z + w
        even.append(shaped(z))
    out_re, out_im = [], []
    for c in range(count):
        odd = shaped(mm(pieces[c], f0))
        u = mm(odd, g0) + mm(even[c], g_right) + mm(even[c + 1], g_left)
        u = u.astype(BF16)
        out_re.append(u[:, :LANES])
        out_im.append(u[:, LANES:])
    return jnp.concatenate(out_re, axis=1), jnp.concatenate(out_im, axis=1)


def centre_kernel(re_ref, im_ref, rows_ref, fwd_ref, inv_ref, u_ref):
    table = rows_ref[...]
    for i in range(re_ref.shape[0]):
        x = jnp.concatenate([re_ref[i], im_ref[i]], axis=0)
        y = mm(table, x).astype(BF16)
        u_re, u_im = spectral(y[:PATCH], y[PATCH:], fwd_ref, inv_ref)
        u_ref[i] = jnp.concatenate([u_re, u_im], axis=0)


def centre(re, im, rows_t, fwd, inv):
    n, rows, cols = re.shape
    g = 2
    whole = lambda a: pl.BlockSpec(a.shape, lambda i: (0,) * a.ndim)
    block = pl.BlockSpec((g, rows, cols), lambda i: (i, 0, 0))
    return pl.pallas_call(
        centre_kernel,
        grid=(n // g,),
        in_specs=[block, block, whole(rows_t), whole(fwd), whole(inv)],
        out_specs=pl.BlockSpec((g, 2 * rows, cols), lambda i: (i, 0, 0)),
        out_shape=jax.ShapeDtypeStruct((n, 2 * rows, cols), BF16),
        compiler_params=pltpu.CompilerParams(vmem_limit_bytes=40 << 20),
        cost_estimate=pl.CostEstimate(
            flops=n * 2 * 64 * 256 * 256 * 26, bytes_accessed=n * rows * cols * 8,
            transcendentals=n * 64 * 2304,
        ),
        name="centre",
    )(re, im, rows_t, fwd, inv)


GROUP = 16


def edges_kernel(
    re_ref, im_ref, up_re, up_im, dn_re, dn_im, u_ref,
    rows_ref, fwd_ref, inv_ref, bc_ref, be_ref, q_ref, keep
):
    g = re_ref.shape[0]
    half = pl.program_id(0) % (GROUP // g)
    for i in range(g):
        x = jnp.concatenate(
            [up_re[i], re_ref[i], dn_re[i], up_im[i], im_ref[i], dn_im[i]], axis=0
        )
        y = mm(rows_ref[...], x).astype(BF16)
        u_re, u_im = spectral(y[: 2 * PATCH], y[2 * PATCH :], fwd_ref, inv_ref)
        f = mm(be_ref[...], jnp.concatenate([u_re, u_im], axis=0)) + mm(bc_ref[...], u_ref[i])
        re, im = f[:PATCH], f[PATCH:]
        q = im * lax.rsqrt(re * re + im * im + 1.0)
        slot = half * g + i
        tiles = q.shape[1] // LANES
        for h in range(2):
            for c in range(tiles):
                keep[h * tiles + c, pl.ds(slot, HALF, stride=GROUP), :] = q[
                    h * HALF : (h + 1) * HALF, c * LANES : (c + 1) * LANES
                ]

    @pl.when(half == GROUP // g - 1)
    def _():
        for t in range(keep.shape[0]):
            block = keep[t].astype(BF16)
            q_ref[:, :, t * LANES : (t + 1) * LANES] = block.reshape(HALF, GROUP, LANES)


def edges(re, im, halos, u, rows_t, fwd, inv, bc, be):
    n, rows, cols = re.shape
    g = 2
    whole = lambda a: pl.BlockSpec(a.shape, lambda i: (0,) * a.ndim)
    block = pl.BlockSpec((g, rows, cols), lambda i: (i, 0, 0))
    halo = pl.BlockSpec((g, HALF, cols), lambda i: (i, 0, 0))
    return pl.pallas_call(
        edges_kernel,
        grid=(n // g,),
        in_specs=[block, block, halo, halo, halo, halo,
                  pl.BlockSpec((g, 2 * rows, cols), lambda i: (i, 0, 0)),
                  whole(rows_t), whole(fwd), whole(inv), whole(bc), whole(be)],
        out_specs=pl.BlockSpec((HALF, GROUP, 2 * cols), lambda i: (0, i // (GROUP // g), 0)),
        out_shape=jax.ShapeDtypeStruct((HALF, n, 2 * cols), BF16),
        scratch_shapes=[pltpu.VMEM((2 * cols // LANES, HALF * GROUP, LANES), F32)],
        compiler_params=pltpu.CompilerParams(vmem_limit_bytes=48 << 20),
        cost_estimate=pl.CostEstimate(
            flops=n * 2 * 64 * 256 * 256 * 60, bytes_accessed=n * rows * cols * 14,
            transcendentals=n * 128 * 2304,
        ),
        name="edges",
    )(re, im, *halos, u, rows_t, fwd, inv, bc, be)


def projection_kernel(pairs_ref, pairs_t_ref, p_ref, g_ref, band, factor, solved):
    nifg = pairs_ref.shape[0]
    first, second = pairs_ref[:, 0:1], pairs_ref[:, 1:2]
    dates = lax.broadcasted_iota(jnp.int32, (nifg, DATE_PAD), 1)
    one = jnp.ones((nifg, DATE_PAD), F32)
    design = jnp.where(dates == second, one, 0.0) - jnp.where(dates == first, one, 0.0)
    g_ref[...] = design.astype(BF16)

    row_date = lax.broadcasted_iota(jnp.int32, (NDATES, nifg), 0)
    is_first = row_date == pairs_t_ref[0:1, :]
    is_either = is_first | (row_date == pairs_t_ref[1:2, :])
    first_t = jnp.where(is_first, 1.0, 0.0).astype(BF16)
    either_t = jnp.where(is_either, 1.0, 0.0).astype(BF16)
    gap = jnp.broadcast_to(second - first, (nifg, LANES))
    degree = mm(either_t, jnp.ones((nifg, LANES), BF16)) + 1.0
    band[...] = jnp.zeros_like(band)
    band[pl.ds(0, NDATES, stride=8), :] = degree
    for j in range(1, BAND + 1):
        match = jnp.where(gap == j, 1.0, 0.0).astype(BF16)
        band[pl.ds(j, NDATES, stride=8), :] = -mm(first_t, match)

    sub = lax.broadcasted_iota(jnp.int32, (8, LANES), 0)
    flat = sub * LANES + lax.broadcasted_iota(jnp.int32, (8, LANES), 1)

    def unit(i):
        return jnp.where(flat == i, 1.0, 0.0)

    def spread(x, j):
        return jnp.broadcast_to(x[j : j + 1, :], (8, LANES))

    def down(i, carry):
        rows, rhs = list(carry[: BAND + 1]), list(carry[BAND + 1 :])
        r, x = rows[0], rhs[0]
        inv = 1.0 / spread(r, 0)
        scaled = r * inv
        at = pl.ds(pl.multiple_of(i * 8, 8), 8)
        factor[at, :] = scaled
        solved[at, :] = x * inv
        for j in range(1, BAND + 1):
            moved = jnp.where(sub <= BAND - j, pltpu.roll(r, 8 - j, axis=0), 0.0)
            rows[j] = rows[j] - (spread(r, j) * moved) * inv
            rhs[j] = rhs[j] - spread(scaled, j) * x
        ahead = i + BAND + 1
        rows = rows[1:] + [band[pl.ds(pl.multiple_of(ahead * 8, 8), 8), :]]
        rhs = rhs[1:] + [unit(ahead)]
        return tuple(rows + rhs)

    start = [band[j * 8 : (j + 1) * 8, :] for j in range(BAND + 1)]
    start += [unit(j) for j in range(BAND + 1)]
    lax.fori_loop(0, NDATES, down, tuple(start), unroll=4)

    def up(t, carry):
        i = NDATES - 1 - t
        at = pl.ds(pl.multiple_of(i * 8, 8), 8)
        l = factor[at, :]
        x = solved[at, :]
        for j in range(BAND, 0, -1):
            x = x - spread(l, j) * carry[j - 1]
        solved[at, :] = x
        return (x,) + carry[:-1]

    zero = band[pl.ds((NDATES + BAND) * 8, 8), :]
    lax.fori_loop(0, NDATES, up, (zero,) * BAND, unroll=8)

    total = jnp.zeros((NDATES, nifg), F32)
    inverse = jnp.concatenate(
        [solved[pl.ds(c, NDATES, stride=8), :] for c in range(DATE_PAD // LANES)], axis=1
    )
    rest = inverse
    for _ in range(3):
        part = rest.astype(BF16)
        rest = rest - part.astype(F32)
        total = total + lax.dot_general(
            part, g_ref[...], (((1,), (1,)), ((), ())), preferred_element_type=F32
        )
    high = total.astype(BF16)
    p_ref[0:NDATES, :] = high
    p_ref[NDATES:, :] = (total - high.astype(F32)).astype(BF16)


def projection(date_pairs):
    nifg = date_pairs.shape[0]
    tail = (NDATES + 2 * BAND + 6) * 8
    return pl.pallas_call(
        projection_kernel,
        out_shape=(
            jax.ShapeDtypeStruct((2 * NDATES, nifg), BF16),
            jax.ShapeDtypeStruct((nifg, DATE_PAD), BF16),
        ),
        scratch_shapes=[
            pltpu.VMEM((tail, LANES), F32),
            pltpu.VMEM((NDATES * 8, LANES), F32),
            pltpu.VMEM((NDATES * 8, LANES), F32),
        ],
        compiler_params=pltpu.CompilerParams(vmem_limit_bytes=40 << 20),
        cost_estimate=pl.CostEstimate(
            flops=20_000_000_000, bytes_accessed=4_000_000, transcendentals=0
        ),
        name="projection",
    )(date_pairs, date_pairs.T)


def invert_kernel(d_ref, p_ref, g_ref, m_ref):
    scaled = d_ref[...].astype(F32) * (1.0 / THRESHOLD)
    width = scaled.shape[1]
    fill = jnp.zeros((DATE_PAD - NDATES, width), BF16)
    series = None
    misfit = scaled
    for step in range(ITERS):
        if step > 0:
            high = series.astype(BF16)
            low = (series - high.astype(F32)).astype(BF16)
            misfit = scaled - (
                mm(g_ref[...], jnp.concatenate([high, fill], axis=0))
                + mm(g_ref[...], jnp.concatenate([low, fill], axis=0))
            )
        clipped = jnp.clip(misfit, -1.0, 1.0).astype(BF16)
        both = mm(p_ref[...], clipped)
        change = both[:NDATES] + both[NDATES:]
        series = change if series is None else series + change
    series = series * THRESHOLD
    tiles = width // LANES
    for t in range(tiles):
        m_ref[pl.ds(pl.program_id(0) * tiles + t, NDATES, stride=8), :] = series[
            :, t * LANES : (t + 1) * LANES
        ]


def invert(sines, p, g):
    nifg, pixels = sines.shape
    width = 256
    return pl.pallas_call(
        invert_kernel,
        grid=(pixels // width,),
        in_specs=[
            pl.BlockSpec((nifg, width), lambda i: (0, i)),
            pl.BlockSpec(p.shape, lambda i: (0, 0)),
            pl.BlockSpec(g.shape, lambda i: (0, 0)),
        ],
        out_specs=pl.BlockSpec((NDATES * 8, LANES), lambda i: (0, 0)),
        out_shape=jax.ShapeDtypeStruct((NDATES * 8, LANES), F32),
        compiler_params=pltpu.CompilerParams(vmem_limit_bytes=48 << 20),
        name="invert",
    )(sines, p, g)


def split3(x):
    high = x.astype(BF16)
    return high, (x - high.astype(F32)).astype(BF16)


def dot3(a, b):
    (ah, al), (bh, bl) = a, b
    return mm(ah, bh) + (mm(ah, bl) + mm(al, bh))


def gather_kernel(got_ref, ch_ref, cl_ref, series_ref, smooth_ref):
    dates, rows, cols = series_ref.shape
    tiles = cols // LANES
    for d in range(dates):
        halves = []
        for h in range(2):
            halves.append(
                jnp.concatenate(
                    [
                        got_ref[pl.ds(d * 8 + h * tiles + c, HALF, stride=dates * 8), :]
                        for c in range(tiles)
                    ],
                    axis=1,
                )
            )
        x = jnp.concatenate(halves, axis=0)
        series_ref[d] = x
        smooth_ref[d] = dot3(split3(x), (ch_ref[...], cl_ref[...]))


def gather(got, col_high, col_low, rows, cols):
    dates = got.shape[0] // 8 // HALF
    return pl.pallas_call(
        gather_kernel,
        out_shape=(jax.ShapeDtypeStruct((dates, rows, cols), F32),) * 2,
        compiler_params=pltpu.CompilerParams(vmem_limit_bytes=40 << 20),
        name="gather",
    )(got, col_high, col_low)


def finish_kernel(where_ref, series_ref, smooth_ref, up_ref, dn_ref, rh_ref, rl_ref, corr_ref, atm_ref):
    table = (rh_ref[0], rl_ref[0])
    for d in range(series_ref.shape[0]):
        x = jnp.concatenate([up_ref[d], smooth_ref[d], dn_ref[d]], axis=0)
        atm = dot3(table, split3(x))
        atm_ref[d] = atm
        corr_ref[d] = series_ref[d] - atm


def finish(where, series, smooth, up, dn, row_high, row_low):
    dates, rows, cols = series.shape
    g = 5
    block = pl.BlockSpec((g, rows, cols), lambda i, w: (i, 0, 0))
    halo = pl.BlockSpec((g, RADIUS, cols), lambda i, w: (i, 0, 0))
    table = pl.BlockSpec((1,) + row_high.shape[1:], lambda i, w: (w[0], 0, 0))
    return pl.pallas_call(
        finish_kernel,
        grid_spec=pltpu.PrefetchScalarGridSpec(
            num_scalar_prefetch=1,
            grid=(dates // g,),
            in_specs=[block, block, halo, halo, table, table],
            out_specs=[block, block],
        ),
        out_shape=(jax.ShapeDtypeStruct((dates, rows, cols), F32),) * 2,
        compiler_params=pltpu.CompilerParams(vmem_limit_bytes=40 << 20),
        name="finish",
    )(where, series, smooth, up, dn, row_high, row_low)


def neighbours(low_part, high_part, axis):
    count = lax.axis_size(axis)
    forward = [(i, i + 1) for i in range(count - 1)]
    backward = [(b, a) for a, b in forward]
    return lax.ppermute(high_part, axis, forward), lax.ppermute(low_part, axis, backward)


def on_device(ifg_real, ifg_imag, date_pairs):
    n, rows, cols = ifg_real.shape
    rows_c, rows_e, fwd, inv, back_c, back_e = (jnp.asarray(t) for t in tables())
    col_t, row_t = blur_tables(rows * lax.axis_size("row"), rows, cols)
    col_high, col_low = bf16(col_t), bf16(col_t - bf16(col_t).astype(np.float32))
    row_high, row_low = bf16(row_t), bf16(row_t - bf16(row_t).astype(np.float32))

    up_re, dn_re = neighbours(ifg_real[:, :HALF], ifg_real[:, rows - HALF :], "row")
    up_im, dn_im = neighbours(ifg_imag[:, :HALF], ifg_imag[:, rows - HALF :], "row")
    u = centre(ifg_real, ifg_imag, rows_c, fwd, inv)
    p, g = projection(date_pairs)
    q = edges(ifg_real, ifg_imag, (up_re, up_im, dn_re, dn_im), u, rows_e, fwd, inv, back_c, back_e)
    sines = lax.all_to_all(q, "ifg", split_axis=0, concat_axis=0, tiled=True)
    series = invert(sines.reshape(-1, 2 * cols), p, g)
    devices = lax.axis_size("ifg")
    series = lax.all_to_all(
        series.reshape(devices, -1, LANES), "ifg", split_axis=0, concat_axis=0, tiled=True
    )
    series, smooth = gather(
        series.reshape(-1, LANES), jnp.asarray(col_high), jnp.asarray(col_low), rows, cols
    )
    up, dn = neighbours(smooth[:, :RADIUS], smooth[:, rows - RADIUS :], "row")
    where = lax.axis_index("row").astype(jnp.int32).reshape(1)
    return finish(where, series, smooth, up, dn, jnp.asarray(row_high), jnp.asarray(row_low))


def solution(mesh):
    placed = (P("ifg", "row", None), P("ifg", "row", None), P())
    return jax.shard_map(
        on_device,
        mesh=mesh,
        in_specs=placed,
        out_specs=(P("ifg", "row", None), P("ifg", "row", None)),
        check_vma=False,
    )
```

```python
import math

import jax
import jax.numpy as jnp
import ml_dtypes
import numpy as np
from jax import lax
from jax.experimental import pallas as pl
from jax.experimental.pallas import tpu as pltpu
from jax.sharding import PartitionSpec as P

PATCH = 64
HALF = PATCH // 2
NDATES = 320
ITERS = 3
RADIUS = 16
SIGMA = 5.0
THRESHOLD = 0.3
BAND = 5
LANES = 128
DATE_PAD = 384
BF16 = jnp.bfloat16
F32 = jnp.float32


def bf16(x):
    return np.asarray(x, np.float32).astype(ml_dtypes.bfloat16)


def tables():
    n = np.arange(PATCH)
    angle = (n[:, None] * n[None, :] % PATCH) * (2.0 * math.pi / PATCH)
    c = bf16(np.cos(angle) / 8.0).astype(np.float64)
    s = bf16(np.sin(angle) / 8.0).astype(np.float64)
    taper = np.sin(math.pi * (n + 0.5) / PATCH) ** 2
    two = np.eye(2)
    zero = np.zeros((PATCH, PATCH))

    rows_strip = np.block([[c, s], [-s, c]])
    c2, s2 = np.kron(two, c), np.kron(two, s)
    cols = np.block([[c2, -s2], [s2, c2]])
    shift = np.zeros((2, LANES, LANES))
    for i in range(LANES):
        if i < HALF:
            shift[0, LANES - HALF + i, i] = 1.0
        else:
            shift[1, i - HALF, i] = 1.0
    left, right = np.kron(two, shift[0]), np.kron(two, shift[1])
    t2 = np.concatenate([taper, taper])
    inv = np.block([[c2 * t2, s2 * t2], [-s2 * t2, c2 * t2]])
    forward = np.stack([cols, left @ cols, right @ cols])
    inverse = np.stack([inv, inv @ left.T, inv @ right.T])
    ct, st = c * taper[:, None], s * taper[:, None]
    back = []
    for centre_rows, edge_rows in ((slice(0, HALF), slice(HALF, PATCH)), (slice(HALF, PATCH), slice(0, HALF))):
        c1, s1, c2, s2 = ct[centre_rows], st[centre_rows], ct[edge_rows], st[edge_rows]
        back.append(np.block([[c1, -s1, c2, -s2], [s1, c1, s2, c2]]))
    return tuple(bf16(x) for x in (rows_strip, forward, inverse, *back))


def gauss(distance):
    return np.where(np.abs(distance) <= RADIUS, np.exp(-0.5 * (distance / SIGMA) ** 2), 0.0)


def blur_tables(rows, local_rows, cols):
    i = np.arange(cols)
    by_col = gauss(i[:, None] - i[None, :])
    by_col = by_col / by_col.sum(0, keepdims=True)
    out = np.arange(rows)[:, None]
    src = np.arange(-RADIUS, rows + RADIUS)[None, :]
    by_row = gauss(src - out) * ((src >= 0) & (src < rows))
    by_row = by_row / by_row.sum(1, keepdims=True)
    blocks = [
        by_row[a : a + local_rows, a : a + local_rows + 2 * RADIUS]
        for a in range(0, rows, local_rows)
    ]
    return by_col.astype(np.float32), np.stack(blocks).astype(np.float32)


def mm(a, b):
    return jnp.dot(a, b, preferred_element_type=F32)


def spectral(y_re, y_im, fwd, inv):
    count = y_re.shape[1] // LANES
    pieces = []
    for c in range(count):
        sl = slice(c * LANES, (c + 1) * LANES)
        pieces.append(jnp.concatenate([y_re[:, sl], y_im[:, sl]], axis=1))
    f0, f_left, f_right = fwd[0], fwd[1], fwd[2]
    g0, g_left, g_right = inv[0], inv[1], inv[2]

    def shaped(z):
        re, im = z[:, :LANES], z[:, LANES:]
        scale = lax.rsqrt(lax.rsqrt(re * re + im * im + 1.0))
        return jnp.concatenate([(re * scale).astype(BF16), (im * scale).astype(BF16)], axis=1)

    even = []
    for c in range(count + 1):
        z = None
        if c > 0:
            z = mm(pieces[c - 1], f_left)
        if c < count:
            w = mm(pieces[c], f_right)
            z = w if z is None else z + w
        even.append(shaped(z))
    out_re, out_im = [], []
    for c in range(count):
        odd = shaped(mm(pieces[c], f0))
        u = mm(odd, g0) + mm(even[c], g_right) + mm(even[c + 1], g_left)
        u = u.astype(BF16)
        out_re.append(u[:, :LANES])
        out_im.append(u[:, LANES:])
    return jnp.concatenate(out_re, axis=1), jnp.concatenate(out_im, axis=1)


def stacked_rows(table, strips):
    y = [mm(table, x).astype(BF16) for x in strips]
    y_re = jnp.concatenate([t[:PATCH] for t in y], axis=0)
    y_im = jnp.concatenate([t[PATCH:] for t in y], axis=0)
    return y_re, y_im


def centre_kernel(re_ref, im_ref, rows_ref, fwd_ref, inv_ref, u_ref):
    n = re_ref.shape[0]
    strips = [jnp.concatenate([re_ref[i], im_ref[i]], axis=0) for i in range(n)]
    y_re, y_im = stacked_rows(rows_ref[...], strips)
    u_re, u_im = spectral(y_re, y_im, fwd_ref, inv_ref)
    for i in range(n):
        sl = slice(i * PATCH, (i + 1) * PATCH)
        u_ref[i, :PATCH] = u_re[sl]
        u_ref[i, PATCH:] = u_im[sl]


BATCH = 4


def in_hbm(x):
    return pltpu.with_memory_space_constraint(x, pltpu.HBM)


def whole(a):
    return pl.BlockSpec(a.shape, lambda i: (0,) * a.ndim)


def centre(re, im, rows_t, fwd, inv):
    n, rows, cols = re.shape
    g = BATCH
    block = pl.BlockSpec((g, rows, cols), lambda i: (i, 0, 0))
    return pl.pallas_call(
        centre_kernel,
        grid=(n // g,),
        in_specs=[block, block, whole(rows_t), whole(fwd), whole(inv)],
        out_specs=pl.BlockSpec((g, 2 * rows, cols), lambda i: (i, 0, 0)),
        out_shape=pltpu.HBM((n, 2 * rows, cols), BF16),
        compiler_params=pltpu.CompilerParams(vmem_limit_bytes=24 << 20),
        cost_estimate=pl.CostEstimate(
            flops=n * 2 * 64 * 256 * 256 * 26, bytes_accessed=n * rows * cols * 8,
            transcendentals=n * 64 * 2304,
        ),
        name="centre",
    )(in_hbm(re), in_hbm(im), rows_t, fwd, inv)


GROUP = 16


def edge_kernel(upper, re_ref, im_ref, halo_ref, u_ref, rows_ref, fwd_ref, inv_ref, back_ref, q_ref, keep):
    g = re_ref.shape[0]
    part = pl.program_id(0) % (GROUP // g)
    strips = []
    for i in range(g):
        own = [re_ref[i], im_ref[i]]
        other = [halo_ref[0, i], halo_ref[1, i]]
        first, second = (other, own) if upper else (own, other)
        strips.append(jnp.concatenate([first[0], second[0], first[1], second[1]], axis=0))
    y_re, y_im = stacked_rows(rows_ref[...], strips)
    u_re, u_im = spectral(y_re, y_im, fwd_ref, inv_ref)
    for i in range(g):
        sl = slice(i * PATCH, (i + 1) * PATCH)
        f = mm(back_ref[...], jnp.concatenate([u_ref[i], u_re[sl], u_im[sl]], axis=0))
        re, im = f[:HALF], f[HALF:]
        q = im * lax.rsqrt(re * re + im * im + 1.0)
        for c in range(keep.shape[0]):
            keep[c, pl.ds(part * g + i, HALF, stride=GROUP), :] = q[:, c * LANES : (c + 1) * LANES]

    @pl.when(part == GROUP // g - 1)
    def _():
        for t in range(keep.shape[0]):
            block = keep[t].astype(BF16)
            q_ref[:, :, t * LANES : (t + 1) * LANES] = block.reshape(HALF, GROUP, LANES)


def edge(upper, re, im, halo, u, rows_t, fwd, inv, back):
    n, rows, cols = re.shape
    g = BATCH
    side = 0 if upper else 1
    block = pl.BlockSpec((g, HALF, cols), lambda i: (i, side, 0))
    return pl.pallas_call(
        lambda *refs: edge_kernel(upper, *refs),
        grid=(n // g,),
        in_specs=[block, block,
                  pl.BlockSpec((2, g, HALF, cols), lambda i: (0, i, 0, 0)),
                  pl.BlockSpec((g, 2 * rows, cols), lambda i: (i, 0, 0)),
                  whole(rows_t), whole(fwd), whole(inv), whole(back)],
        out_specs=pl.BlockSpec((HALF, GROUP, cols), lambda i: (0, i // (GROUP // g), 0)),
        out_shape=pltpu.HBM((HALF, n, cols), BF16),
        scratch_shapes=[pltpu.VMEM((cols // LANES, HALF * GROUP, LANES), F32)],
        compiler_params=pltpu.CompilerParams(vmem_limit_bytes=24 << 20),
        cost_estimate=pl.CostEstimate(
            flops=n * 2 * 64 * 256 * 256 * 30, bytes_accessed=n * rows * cols * 7,
            transcendentals=n * 64 * 2304,
        ),
        name="upper" if upper else "lower",
    )(in_hbm(re), in_hbm(im), halo, in_hbm(u), rows_t, fwd, inv, back)


def projection_kernel(pairs_ref, pairs_t_ref, p_ref, g_ref, band, factor, solved):
    nifg = pairs_ref.shape[0]
    first, second = pairs_ref[:, 0:1], pairs_ref[:, 1:2]
    def design(width, wrap):
        dates = lax.broadcasted_iota(jnp.int32, (nifg, width), 1)
        if wrap:
            dates = jnp.where(dates >= NDATES, dates - NDATES, dates)
        return (jnp.where(dates == second, 1.0, 0.0) - jnp.where(dates == first, 1.0, 0.0)).astype(BF16)

    g_ref[...] = design(2 * NDATES, True)
    single = design(DATE_PAD, False)

    row_date = lax.broadcasted_iota(jnp.int32, (NDATES, nifg), 0)
    is_first = row_date == pairs_t_ref[0:1, :]
    is_either = is_first | (row_date == pairs_t_ref[1:2, :])
    first_t = jnp.where(is_first, 1.0, 0.0).astype(BF16)
    either_t = jnp.where(is_either, 1.0, 0.0).astype(BF16)
    gap = jnp.broadcast_to(second - first, (nifg, LANES))
    degree = mm(either_t, jnp.ones((nifg, LANES), BF16)) + 1.0
    band[...] = jnp.zeros_like(band)
    band[pl.ds(0, NDATES, stride=8), :] = degree
    for j in range(1, BAND + 1):
        match = jnp.where(gap == j, 1.0, 0.0).astype(BF16)
        band[pl.ds(j, NDATES, stride=8), :] = -mm(first_t, match)

    sub = lax.broadcasted_iota(jnp.int32, (8, LANES), 0)
    flat = sub * LANES + lax.broadcasted_iota(jnp.int32, (8, LANES), 1)

    def unit(i):
        return jnp.where(flat == i, 1.0, 0.0)

    def spread(x, j):
        return jnp.broadcast_to(x[j : j + 1, :], (8, LANES))

    def down(i, carry):
        rows, rhs = list(carry[: BAND + 1]), list(carry[BAND + 1 :])
        r, x = rows[0], rhs[0]
        inv = 1.0 / spread(r, 0)
        scaled = r * inv
        at = pl.ds(pl.multiple_of(i * 8, 8), 8)
        factor[at, :] = scaled
        solved[at, :] = x * inv
        for j in range(1, BAND + 1):
            moved = jnp.where(sub <= BAND - j, pltpu.roll(r, 8 - j, axis=0), 0.0)
            rows[j] = rows[j] - (spread(r, j) * moved) * inv
            rhs[j] = rhs[j] - spread(scaled, j) * x
        ahead = i + BAND + 1
        rows = rows[1:] + [band[pl.ds(pl.multiple_of(ahead * 8, 8), 8), :]]
        rhs = rhs[1:] + [unit(ahead)]
        return tuple(rows + rhs)

    start = [band[j * 8 : (j + 1) * 8, :] for j in range(BAND + 1)]
    start += [unit(j) for j in range(BAND + 1)]
    lax.fori_loop(0, NDATES, down, tuple(start), unroll=4)

    def up(t, carry):
        i = NDATES - 1 - t
        at = pl.ds(pl.multiple_of(i * 8, 8), 8)
        l = factor[at, :]
        x = solved[at, :]
        for j in range(BAND, 0, -1):
            x = x - spread(l, j) * carry[j - 1]
        solved[at, :] = x
        return (x,) + carry[:-1]

    zero = band[pl.ds((NDATES + BAND) * 8, 8), :]
    lax.fori_loop(0, NDATES, up, (zero,) * BAND, unroll=8)

    total = jnp.zeros((NDATES, nifg), F32)
    inverse = jnp.concatenate(
        [solved[pl.ds(c, NDATES, stride=8), :] for c in range(DATE_PAD // LANES)], axis=1
    )
    rest = inverse
    for _ in range(3):
        part = rest.astype(BF16)
        rest = rest - part.astype(F32)
        total = total + lax.dot_general(
            part, single, (((1,), (1,)), ((), ())), preferred_element_type=F32
        )
    high = total.astype(BF16)
    p_ref[...] = high


def projection(date_pairs):
    nifg = date_pairs.shape[0]
    tail = (NDATES + 2 * BAND + 6) * 8
    return pl.pallas_call(
        projection_kernel,
        out_shape=(
            pltpu.HBM((NDATES, nifg), BF16),
            pltpu.HBM((nifg, 2 * NDATES), BF16),
        ),
        scratch_shapes=[
            pltpu.VMEM((tail, LANES), F32),
            pltpu.VMEM((NDATES * 8, LANES), F32),
            pltpu.VMEM((NDATES * 8, LANES), F32),
        ],
        compiler_params=pltpu.CompilerParams(vmem_limit_bytes=40 << 20),
        cost_estimate=pl.CostEstimate(
            flops=20_000_000_000, bytes_accessed=4_000_000, transcendentals=0
        ),
        name="projection",
    )(date_pairs, date_pairs.T)


def invert_kernel(d_ref, p_ref, g_ref, *refs):
    scaled = d_ref[...].astype(F32) * (1.0 / THRESHOLD)
    series = None
    misfit = scaled
    for step in range(ITERS):
        if step > 0:
            high = series.astype(BF16)
            low = (series - high.astype(F32)).astype(BF16)
            misfit = scaled - mm(g_ref[...], jnp.concatenate([high, low], axis=0))
        clipped = jnp.clip(misfit, -1.0, 1.0).astype(BF16)
        change = mm(p_ref[...], clipped)
        series = change if series is None else series + change
    series = series * THRESHOLD
    tiles = series.shape[1] // LANES
    place = pl.program_id(0) * tiles
    if len(refs) == 1:
        (m_ref,) = refs
        for t in range(tiles):
            m_ref[pl.ds(place + t, NDATES, stride=4), :] = series[:, t * LANES : (t + 1) * LANES]
        return
    other_ref, m_ref, keep = refs
    for t in range(tiles):
        keep[pl.ds(4 + place + t, NDATES, stride=8), :] = series[:, t * LANES : (t + 1) * LANES]

    @pl.when(pl.program_id(0) == pl.num_programs(0) - 1)
    def _():
        for t in range(4):
            keep[pl.ds(t, NDATES, stride=8), :] = other_ref[pl.ds(t, NDATES, stride=4), :]
        m_ref[...] = keep[...].astype(BF16)


WIDTH = 256


def invert(sines, p, g, *other):
    nifg, pixels = sines.shape
    width = WIDTH
    rows = NDATES * (8 if other else 4)
    return pl.pallas_call(
        invert_kernel,
        grid=(pixels // width,),
        in_specs=[
            pl.BlockSpec((nifg, width), lambda i: (0, i)),
            whole(p), whole(g), *(whole(x) for x in other)
        ],
        out_specs=pl.BlockSpec((rows, LANES), lambda i: (0, 0)),
        out_shape=jax.ShapeDtypeStruct((rows, LANES), BF16) if other else pltpu.HBM((rows, LANES), F32),
        scratch_shapes=[pltpu.VMEM((rows, LANES), F32)] if other else [],
        compiler_params=pltpu.CompilerParams(vmem_limit_bytes=32 << 20),
        cost_estimate=pl.CostEstimate(
            flops=pixels * nifg * NDATES * 14, bytes_accessed=6_000_000, transcendentals=0
        ),
        name="invert_rest" if other else "invert",
    )(sines, in_hbm(p), in_hbm(g), *(in_hbm(x) for x in other))


def split3(x):
    high = x.astype(BF16)
    return high, (x - high.astype(F32)).astype(BF16)


def dot3(a, b):
    (ah, al), (bh, bl) = a, b
    return mm(ah, bh) + (mm(ah, bl) + mm(al, bh))


def gather_kernel(got_ref, ch_ref, cl_ref, series_ref, smooth_ref, low_ref, high_ref, wide):
    dates, rows, cols = series_ref.shape
    tiles = cols // LANES
    wide[...] = got_ref[...].astype(F32)
    for d in range(dates):
        halves = []
        for h in range(2):
            halves.append(
                jnp.concatenate(
                    [
                        wide[pl.ds(d * 8 + h * tiles + c, HALF, stride=dates * 8), :]
                        for c in range(tiles)
                    ],
                    axis=1,
                )
            )
        x = jnp.concatenate(halves, axis=0)
        series_ref[d] = x
        x = x.astype(BF16)
        smooth = mm(x, ch_ref[...]) + mm(x, cl_ref[...])
        smooth_ref[d] = smooth
        low_ref[d] = smooth[:RADIUS]
        high_ref[d] = smooth[rows - RADIUS :]


def gather(got, col_high, col_low, rows, cols):
    dates = got.shape[0] // 8 // HALF
    block = jax.ShapeDtypeStruct((dates, rows, cols), F32)
    border = jax.ShapeDtypeStruct((dates, RADIUS, cols), F32)
    return pl.pallas_call(
        gather_kernel,
        out_shape=(block, block, border, border),
        scratch_shapes=[pltpu.VMEM(got.shape, F32)],
        compiler_params=pltpu.CompilerParams(vmem_limit_bytes=24 << 20),
        name="gather",
    )(got, col_high, col_low)


def finish_kernel(where_ref, series_ref, smooth_ref, up_ref, dn_ref, rh_ref, rl_ref, corr_ref, atm_ref):
    table = (rh_ref[0], rl_ref[0])
    for d in range(series_ref.shape[0]):
        x = jnp.concatenate([up_ref[d], smooth_ref[d], dn_ref[d]], axis=0)
        atm = dot3(table, split3(x))
        atm_ref[d] = atm
        corr_ref[d] = series_ref[d] - atm


def finish(where, series, smooth, up, dn, row_high, row_low):
    dates, rows, cols = series.shape
    g = 5
    block = pl.BlockSpec((g, rows, cols), lambda i, w: (i, 0, 0))
    halo = pl.BlockSpec((g, RADIUS, cols), lambda i, w: (i, 0, 0))
    table = pl.BlockSpec((1,) + row_high.shape[1:], lambda i, w: (w[0], 0, 0))
    return pl.pallas_call(
        finish_kernel,
        grid_spec=pltpu.PrefetchScalarGridSpec(
            num_scalar_prefetch=1,
            grid=(dates // g,),
            in_specs=[block, block, halo, halo, table, table],
            out_specs=[block, block],
        ),
        out_shape=(jax.ShapeDtypeStruct((dates, rows, cols), F32),) * 2,
        compiler_params=pltpu.CompilerParams(vmem_limit_bytes=40 << 20),
        name="finish",
    )(where, series, smooth, up, dn, row_high, row_low)


def neighbours(low_part, high_part, axis):
    count = lax.axis_size(axis)
    forward = [(i, i + 1) for i in range(count - 1)]
    backward = [(b, a) for a, b in forward]
    return lax.ppermute(high_part, axis, forward), lax.ppermute(low_part, axis, backward)


def on_device(ifg_real, ifg_imag, date_pairs):
    n, rows, cols = ifg_real.shape
    rows_t, fwd, inv, back_up, back_dn = (jnp.asarray(t) for t in tables())
    col_t, row_t = blur_tables(rows * lax.axis_size("row"), rows, cols)
    col_high, col_low = bf16(col_t), bf16(col_t - bf16(col_t).astype(np.float32))
    row_high, row_low = bf16(row_t), bf16(row_t - bf16(row_t).astype(np.float32))

    low = jnp.stack([ifg_real[:, :HALF], ifg_imag[:, :HALF]])
    high = jnp.stack([ifg_real[:, rows - HALF :], ifg_imag[:, rows - HALF :]])
    above, below = neighbours(low, high, "row")
    u = centre(ifg_real, ifg_imag, rows_t, fwd, inv)
    p, g = projection(date_pairs)
    u, p, g = lax.optimization_barrier((u, p, g))
    series = ()
    for upper, halo, back in ((True, above, back_up), (False, below, back_dn)):
        q = edge(upper, ifg_real, ifg_imag, halo, u, rows_t, fwd, inv, back)
        sines = lax.all_to_all(q, "ifg", split_axis=0, concat_axis=0, tiled=True)
        series = (invert(sines.reshape(-1, cols), p, g, *series),)
    devices = lax.axis_size("ifg")
    series = lax.all_to_all(
        series[0].reshape(devices, -1, LANES), "ifg", split_axis=0, concat_axis=0, tiled=True
    )
    series, smooth, low, high = gather(
        series.reshape(-1, LANES), jnp.asarray(col_high), jnp.asarray(col_low), rows, cols
    )
    up, dn = neighbours(low, high, "row")
    where = lax.axis_index("row").astype(jnp.int32).reshape(1)
    return finish(where, series, smooth, up, dn, jnp.asarray(row_high), jnp.asarray(row_low))


def solution(mesh):
    placed = (P("ifg", "row", None), P("ifg", "row", None), P())
    return jax.shard_map(
        on_device,
        mesh=mesh,
        in_specs=placed,
        out_specs=(P("ifg", "row", None), P("ifg", "row", None)),
        check_vma=False,
    )
```

```python
import math

import jax
import jax.numpy as jnp
import ml_dtypes
import numpy as np
from jax import lax
from jax.experimental import pallas as pl
from jax.experimental.pallas import tpu as pltpu
from jax.sharding import PartitionSpec as P

PATCH = 64
HALF = PATCH // 2
NDATES = 320
ITERS = 3
RADIUS = 16
SIGMA = 5.0
THRESHOLD = 0.3
BAND = 5
LANES = 128
DATE_PAD = 384
BF16 = jnp.bfloat16
F32 = jnp.float32


def bf16(x):
    return np.asarray(x, np.float32).astype(ml_dtypes.bfloat16)


def tables():
    n = np.arange(PATCH)
    angle = (n[:, None] * n[None, :] % PATCH) * (2.0 * math.pi / PATCH)
    c = bf16(np.cos(angle) / 8.0).astype(np.float64)
    s = bf16(np.sin(angle) / 8.0).astype(np.float64)
    taper = np.sin(math.pi * (n + 0.5) / PATCH) ** 2
    two = np.eye(2)
    zero = np.zeros((PATCH, PATCH))

    rows_strip = np.block([[c, s], [-s, c]])
    c2, s2 = np.kron(two, c), np.kron(two, s)
    forward = np.block([[c2, -s2], [s2, c2]])
    t2 = np.concatenate([taper, taper])
    inverse = np.block([[c2 * t2, s2 * t2], [-s2 * t2, c2 * t2]])
    ct, st = c * taper[:, None], s * taper[:, None]
    back = []
    for centre_rows, edge_rows in ((slice(0, HALF), slice(HALF, PATCH)), (slice(HALF, PATCH), slice(0, HALF))):
        c1, s1, c2, s2 = ct[centre_rows], st[centre_rows], ct[edge_rows], st[edge_rows]
        back.append(np.block([[c1, -s1, c2, -s2], [s1, c1, s2, c2]]))
    return tuple(bf16(x) for x in (rows_strip, forward, inverse, *back))


def gauss(distance):
    return np.where(np.abs(distance) <= RADIUS, np.exp(-0.5 * (distance / SIGMA) ** 2), 0.0)


def blur_tables(rows, local_rows, cols):
    i = np.arange(cols)
    by_col = gauss(i[:, None] - i[None, :])
    by_col = by_col / by_col.sum(0, keepdims=True)
    out = np.arange(rows)[:, None]
    src = np.arange(-RADIUS, rows + RADIUS)[None, :]
    by_row = gauss(src - out) * ((src >= 0) & (src < rows))
    by_row = by_row / by_row.sum(1, keepdims=True)
    blocks = [
        by_row[a : a + local_rows, a : a + local_rows + 2 * RADIUS]
        for a in range(0, rows, local_rows)
    ]
    return by_col.astype(np.float32), np.stack(blocks).astype(np.float32)


def mm(a, b):
    return jnp.dot(a, b, preferred_element_type=F32)


def spectral(y_re, y_im, fwd, inv):
    count = y_re.shape[1] // LANES
    pieces = []
    for c in range(count):
        sl = slice(c * LANES, (c + 1) * LANES)
        pieces.append(jnp.concatenate([y_re[:, sl], y_im[:, sl]], axis=1))
    f0, g0 = fwd[...], inv[...]

    def shaped(z):
        re, im = z[:, :LANES], z[:, LANES:]
        scale = lax.rsqrt(lax.rsqrt(re * re + im * im + 1.0))
        return jnp.concatenate([(re * scale).astype(BF16), (im * scale).astype(BF16)], axis=1)

    lane = lax.broadcasted_iota(jnp.int32, (y_re.shape[0], LANES), 1)

    def moved(y):
        rolled = [pltpu.roll(y[:, c * LANES : (c + 1) * LANES], HALF, axis=1) for c in range(count)]
        zero = jnp.zeros_like(rolled[0])
        before, after = [zero] + rolled, rolled + [zero]
        return [jnp.where(lane < HALF, a, b) for a, b in zip(before, after)]

    even = [
        shaped(mm(jnp.concatenate([a, b], axis=1), f0)) for a, b in zip(moved(y_re), moved(y_im))
    ]
    def back(z):
        u = mm(z, g0)
        return [pltpu.roll(u[:, :LANES], LANES - HALF, axis=1), pltpu.roll(u[:, LANES:], LANES - HALF, axis=1)]

    turned = [back(z) for z in even]
    out_re, out_im = [], []
    for c in range(count):
        u = mm(shaped(mm(pieces[c], f0)), g0)
        for out, k in ((out_re, 0), (out_im, 1)):
            other = jnp.where(lane < LANES - HALF, turned[c][k], turned[c + 1][k])
            out.append((u[:, k * LANES : (k + 1) * LANES] + other).astype(BF16))
    return jnp.concatenate(out_re, axis=1), jnp.concatenate(out_im, axis=1)


def stacked_rows(table, strips):
    y = [mm(table, x).astype(BF16) for x in strips]
    y_re = jnp.concatenate([t[:PATCH] for t in y], axis=0)
    y_im = jnp.concatenate([t[PATCH:] for t in y], axis=0)
    return y_re, y_im


def centre_kernel(re_ref, im_ref, rows_ref, fwd_ref, inv_ref, u_ref):
    n = re_ref.shape[0]
    strips = [jnp.concatenate([re_ref[i], im_ref[i]], axis=0) for i in range(n)]
    y_re, y_im = stacked_rows(rows_ref[...], strips)
    u_re, u_im = spectral(y_re, y_im, fwd_ref, inv_ref)
    for i in range(n):
        sl = slice(i * PATCH, (i + 1) * PATCH)
        u_ref[i, :PATCH] = u_re[sl]
        u_ref[i, PATCH:] = u_im[sl]


BATCH = 8


def in_hbm(x):
    return pltpu.with_memory_space_constraint(x, pltpu.HBM)


def whole(a):
    return pl.BlockSpec(a.shape, lambda i: (0,) * a.ndim)


def centre(re, im, rows_t, fwd, inv):
    n, rows, cols = re.shape
    g = BATCH
    block = pl.BlockSpec((g, rows, cols), lambda i: (i, 0, 0))
    return pl.pallas_call(
        centre_kernel,
        grid=(n // g,),
        in_specs=[block, block, whole(rows_t), whole(fwd), whole(inv)],
        out_specs=pl.BlockSpec((g, 2 * rows, cols), lambda i: (i, 0, 0)),
        out_shape=pltpu.HBM((n, 2 * rows, cols), BF16),
        compiler_params=pltpu.CompilerParams(vmem_limit_bytes=24 << 20),
        cost_estimate=pl.CostEstimate(
            flops=n * 2 * 64 * 256 * 256 * 26, bytes_accessed=n * rows * cols * 8,
            transcendentals=n * 64 * 2304,
        ),
        name="centre",
    )(*(in_hbm(x) for x in (re, im, rows_t, fwd, inv)))


GROUP = 16


def edge_kernel(upper, re_ref, im_ref, halo_ref, u_ref, rows_ref, fwd_ref, inv_ref, back_ref, q_ref, keep):
    g = re_ref.shape[0]
    part = pl.program_id(0) % (GROUP // g)
    strips = []
    for i in range(g):
        own = [re_ref[i], im_ref[i]]
        other = [halo_ref[0, i], halo_ref[1, i]]
        first, second = (other, own) if upper else (own, other)
        strips.append(jnp.concatenate([first[0], second[0], first[1], second[1]], axis=0))
    y_re, y_im = stacked_rows(rows_ref[...], strips)
    u_re, u_im = spectral(y_re, y_im, fwd_ref, inv_ref)
    for i in range(g):
        sl = slice(i * PATCH, (i + 1) * PATCH)
        f = mm(back_ref[...], jnp.concatenate([u_ref[i], u_re[sl], u_im[sl]], axis=0))
        re, im = f[:HALF], f[HALF:]
        q = im * lax.rsqrt(re * re + im * im + 1.0)
        for c in range(keep.shape[0]):
            keep[c, pl.ds(part * g + i, HALF, stride=GROUP), :] = q[:, c * LANES : (c + 1) * LANES]

    @pl.when(part == GROUP // g - 1)
    def _():
        for t in range(keep.shape[0]):
            block = keep[t].astype(BF16)
            q_ref[:, :, t * LANES : (t + 1) * LANES] = block.reshape(HALF, GROUP, LANES)


def edge(upper, re, im, halo, u, rows_t, fwd, inv, back):
    n, rows, cols = re.shape
    g = BATCH
    side = 0 if upper else 1
    block = pl.BlockSpec((g, HALF, cols), lambda i: (i, side, 0))
    return pl.pallas_call(
        lambda *refs: edge_kernel(upper, *refs),
        grid=(n // g,),
        in_specs=[block, block,
                  pl.BlockSpec((2, g, HALF, cols), lambda i: (0, i, 0, 0)),
                  pl.BlockSpec((g, 2 * rows, cols), lambda i: (i, 0, 0)),
                  whole(rows_t), whole(fwd), whole(inv), whole(back)],
        out_specs=pl.BlockSpec((HALF, GROUP, cols), lambda i: (0, i // (GROUP // g), 0)),
        out_shape=pltpu.HBM((HALF, n, cols), BF16),
        scratch_shapes=[pltpu.VMEM((cols // LANES, HALF * GROUP, LANES), F32)],
        compiler_params=pltpu.CompilerParams(vmem_limit_bytes=24 << 20),
        cost_estimate=pl.CostEstimate(
            flops=n * 2 * 64 * 256 * 256 * 30, bytes_accessed=n * rows * cols * 7,
            transcendentals=n * 64 * 2304,
        ),
        name="upper" if upper else "lower",
    )(in_hbm(re), in_hbm(im), halo, *(in_hbm(x) for x in (u, rows_t, fwd, inv, back)))


def projection_kernel(pairs_ref, pairs_t_ref, p_ref, g_ref, band, factor, solved):
    nifg = pairs_ref.shape[0]
    first, second = pairs_ref[:, 0:1], pairs_ref[:, 1:2]
    def design(width, wrap):
        dates = lax.broadcasted_iota(jnp.int32, (nifg, width), 1)
        if wrap:
            dates = jnp.where(dates >= NDATES, dates - NDATES, dates)
        return (jnp.where(dates == second, 1.0, 0.0) - jnp.where(dates == first, 1.0, 0.0)).astype(BF16)

    g_ref[...] = design(2 * NDATES, True)
    single = design(DATE_PAD, False)

    row_date = lax.broadcasted_iota(jnp.int32, (NDATES, nifg), 0)
    is_first = row_date == pairs_t_ref[0:1, :]
    is_either = is_first | (row_date == pairs_t_ref[1:2, :])
    first_t = jnp.where(is_first, 1.0, 0.0).astype(BF16)
    either_t = jnp.where(is_either, 1.0, 0.0).astype(BF16)
    gap = jnp.broadcast_to(second - first, (nifg, LANES))
    degree = mm(either_t, jnp.ones((nifg, LANES), BF16)) + 1.0
    band[...] = jnp.zeros_like(band)
    band[pl.ds(0, NDATES, stride=8), :] = degree
    for j in range(1, BAND + 1):
        match = jnp.where(gap == j, 1.0, 0.0).astype(BF16)
        band[pl.ds(j, NDATES, stride=8), :] = -mm(first_t, match)

    sub = lax.broadcasted_iota(jnp.int32, (8, LANES), 0)
    flat = sub * LANES + lax.broadcasted_iota(jnp.int32, (8, LANES), 1)

    def unit(i):
        return jnp.where(flat == i, 1.0, 0.0)

    def spread(x, j):
        return jnp.broadcast_to(x[j : j + 1, :], (8, LANES))

    def down(i, carry):
        rows, rhs = list(carry[: BAND + 1]), list(carry[BAND + 1 :])
        r, x = rows[0], rhs[0]
        inv = 1.0 / spread(r, 0)
        scaled = r * inv
        at = pl.ds(pl.multiple_of(i * 8, 8), 8)
        factor[at, :] = scaled
        solved[at, :] = x * inv
        for j in range(1, BAND + 1):
            moved = jnp.where(sub <= BAND - j, pltpu.roll(r, 8 - j, axis=0), 0.0)
            rows[j] = rows[j] - (spread(r, j) * moved) * inv
            rhs[j] = rhs[j] - spread(scaled, j) * x
        ahead = i + BAND + 1
        rows = rows[1:] + [band[pl.ds(pl.multiple_of(ahead * 8, 8), 8), :]]
        rhs = rhs[1:] + [unit(ahead)]
        return tuple(rows + rhs)

    start = [band[j * 8 : (j + 1) * 8, :] for j in range(BAND + 1)]
    start += [unit(j) for j in range(BAND + 1)]
    lax.fori_loop(0, NDATES, down, tuple(start), unroll=4)

    def up(t, carry):
        i = NDATES - 1 - t
        at = pl.ds(pl.multiple_of(i * 8, 8), 8)
        l = factor[at, :]
        x = solved[at, :]
        for j in range(BAND, 0, -1):
            x = x - spread(l, j) * carry[j - 1]
        solved[at, :] = x
        return (x,) + carry[:-1]

    zero = band[pl.ds((NDATES + BAND) * 8, 8), :]
    lax.fori_loop(0, NDATES, up, (zero,) * BAND, unroll=8)

    total = jnp.zeros((NDATES, nifg), F32)
    inverse = jnp.concatenate(
        [solved[pl.ds(c, NDATES, stride=8), :] for c in range(DATE_PAD // LANES)], axis=1
    )
    rest = inverse
    for _ in range(3):
        part = rest.astype(BF16)
        rest = rest - part.astype(F32)
        total = total + lax.dot_general(
            part, single, (((1,), (1,)), ((), ())), preferred_element_type=F32
        )
    high = total.astype(BF16)
    p_ref[...] = high


def projection(date_pairs):
    nifg = date_pairs.shape[0]
    tail = (NDATES + 2 * BAND + 6) * 8
    return pl.pallas_call(
        projection_kernel,
        out_shape=(
            pltpu.HBM((NDATES, nifg), BF16),
            pltpu.HBM((nifg, 2 * NDATES), BF16),
        ),
        scratch_shapes=[
            pltpu.VMEM((tail, LANES), F32),
            pltpu.VMEM((NDATES * 8, LANES), F32),
            pltpu.VMEM((NDATES * 8, LANES), F32),
        ],
        compiler_params=pltpu.CompilerParams(vmem_limit_bytes=40 << 20),
        cost_estimate=pl.CostEstimate(
            flops=20_000_000_000, bytes_accessed=4_000_000, transcendentals=0
        ),
        name="projection",
    )(date_pairs, date_pairs.T)


def invert_kernel(d_ref, p_ref, g_ref, *refs):
    chains = range(d_ref.shape[1] // CHAIN)
    scaled = [d_ref[:, k * CHAIN : (k + 1) * CHAIN].astype(F32) * (1.0 / THRESHOLD) for k in chains]
    series = [None for k in chains]
    misfit = scaled
    for step in range(ITERS):
        if step > 0:
            parts = []
            for k in chains:
                high = series[k].astype(BF16)
                low = (series[k] - high.astype(F32)).astype(BF16)
                parts.append(jnp.concatenate([high, low], axis=0))
            misfit = [scaled[k] - mm(g_ref[...], parts[k]) for k in chains]
        change = [mm(p_ref[...], jnp.clip(misfit[k], -1.0, 1.0).astype(BF16)) for k in chains]
        series = [change[k] if step == 0 else series[k] + change[k] for k in chains]
    series = jnp.concatenate(series, axis=1) * THRESHOLD
    tiles = series.shape[1] // LANES
    place = pl.program_id(0) * tiles
    if len(refs) == 1:
        (m_ref,) = refs
        for t in range(tiles):
            m_ref[pl.ds(place + t, NDATES, stride=4), :] = series[:, t * LANES : (t + 1) * LANES]
        return
    other_ref, m_ref, keep = refs
    for t in range(tiles):
        keep[pl.ds(4 + place + t, NDATES, stride=8), :] = series[:, t * LANES : (t + 1) * LANES]

    @pl.when(pl.program_id(0) == pl.num_programs(0) - 1)
    def _():
        for t in range(4):
            keep[pl.ds(t, NDATES, stride=8), :] = other_ref[pl.ds(t, NDATES, stride=4), :]
        m_ref[...] = keep[...].astype(BF16)


WIDTH = 512
CHAIN = 512


def invert(sines, p, g, *other):
    nifg, pixels = sines.shape
    width = WIDTH
    rows = NDATES * (8 if other else 4)
    return pl.pallas_call(
        invert_kernel,
        grid=(pixels // width,),
        in_specs=[
            pl.BlockSpec((nifg, width), lambda i: (0, i)),
            whole(p), whole(g), *(whole(x) for x in other)
        ],
        out_specs=pl.BlockSpec((rows, LANES), lambda i: (0, 0)),
        out_shape=jax.ShapeDtypeStruct((rows, LANES), BF16) if other else pltpu.HBM((rows, LANES), F32),
        scratch_shapes=[pltpu.VMEM((rows, LANES), F32)] if other else [],
        compiler_params=pltpu.CompilerParams(vmem_limit_bytes=32 << 20),
        cost_estimate=pl.CostEstimate(
            flops=pixels * nifg * NDATES * 14, bytes_accessed=6_000_000, transcendentals=0
        ),
        name="invert_rest" if other else "invert",
    )(sines, in_hbm(p), in_hbm(g), *(in_hbm(x) for x in other))


def halves(table):
    high = bf16(table)
    return jnp.asarray(high), jnp.asarray(bf16(table - high.astype(np.float32)))


def split2(x):
    high = x.astype(BF16)
    return high, (x - high.astype(F32)).astype(BF16)


def dot3(a, b):
    (ah, al), (bh, bl) = a, b
    return mm(ah, bh) + (mm(ah, bl) + mm(al, bh))


def gather_kernel(got_ref, ch_ref, cl_ref, series_ref, smooth_ref, low_ref, high_ref, wide):
    dates, rows, cols = series_ref.shape
    tiles = cols // LANES
    wide[...] = got_ref[...].astype(F32)
    for d in range(dates):
        halves = []
        for h in range(2):
            halves.append(
                jnp.concatenate(
                    [
                        wide[pl.ds(d * 8 + h * tiles + c, HALF, stride=dates * 8), :]
                        for c in range(tiles)
                    ],
                    axis=1,
                )
            )
        x = jnp.concatenate(halves, axis=0)
        series_ref[d] = x
        x = x.astype(BF16)
        smooth = mm(x, ch_ref[...]) + mm(x, cl_ref[...])
        smooth_ref[d] = smooth
        low_ref[d] = smooth[:RADIUS].astype(BF16)
        high_ref[d] = smooth[rows - RADIUS :].astype(BF16)


def gather(got, col_high, col_low, rows, cols):
    dates = got.shape[0] // 8 // HALF
    block = jax.ShapeDtypeStruct((dates, rows, cols), F32)
    border = jax.ShapeDtypeStruct((dates, RADIUS, cols), BF16)
    return pl.pallas_call(
        gather_kernel,
        out_shape=(block, block, border, border),
        scratch_shapes=[pltpu.VMEM(got.shape, F32)],
        compiler_params=pltpu.CompilerParams(vmem_limit_bytes=24 << 20),
        name="gather",
    )(got, col_high, col_low)


def inner_kernel(where_ref, series_ref, smooth_ref, high_ref, low_ref, corr_ref, atm_ref):
    table = (high_ref[0], low_ref[0])
    for d in range(series_ref.shape[0]):
        atm = dot3(table, split2(smooth_ref[d]))
        atm_ref[d] = atm
        corr_ref[d] = series_ref[d] - atm


def inner(where, series, smooth, high, low):
    dates, rows, cols = series.shape
    g = 5
    block = pl.BlockSpec((g, rows, cols), lambda i, w: (i, 0, 0))
    table = pl.BlockSpec((1,) + high.shape[1:], lambda i, w: (w[0], 0, 0))
    return pl.pallas_call(
        inner_kernel,
        grid_spec=pltpu.PrefetchScalarGridSpec(
            num_scalar_prefetch=1,
            grid=(dates // g,),
            in_specs=[block, block, table, table],
            out_specs=[block, block],
        ),
        out_shape=(pltpu.HBM((dates, rows, cols), F32),) * 2,
        compiler_params=pltpu.CompilerParams(vmem_limit_bytes=24 << 20),
        cost_estimate=pl.CostEstimate(
            flops=dates * rows * cols * 1024, bytes_accessed=dates * rows * cols * 16, transcendentals=0
        ),
        name="inner",
    )(where, series, smooth, high, low)


def border_kernel(where_ref, corr_in, atm_in, up_ref, dn_ref, high_ref, low_ref, corr_ref, atm_ref):
    def add(halo_ref):
        for d in range(corr_in.shape[0]):
            x = halo_ref[d]
            more = mm(high_ref[0, 0], x) + mm(low_ref[0, 0], x)
            atm_ref[d] = atm_in[d] + more
            corr_ref[d] = corr_in[d] - more

    @pl.when(pl.program_id(0) == 0)
    def _():
        add(up_ref)

    @pl.when(pl.program_id(0) == 1)
    def _():
        add(dn_ref)


def border(where, corrected, atmosphere, up, dn, high, low):
    dates, rows, cols = corrected.shape
    last = rows // RADIUS - 1
    block = pl.BlockSpec((dates, RADIUS, cols), lambda i, w: (0, i * last, 0))
    halo = pl.BlockSpec(up.shape, lambda i, w: (0, 0, 0))
    table = pl.BlockSpec((1, 1) + high.shape[2:], lambda i, w: (w[0], i, 0, 0))
    return pl.pallas_call(
        border_kernel,
        grid_spec=pltpu.PrefetchScalarGridSpec(
            num_scalar_prefetch=1,
            grid=(2,),
            in_specs=[block, block, halo, halo, table, table],
            out_specs=[block, block],
        ),
        out_shape=(pltpu.HBM((dates, rows, cols), F32),) * 2,
        input_output_aliases={1: 0, 2: 1},
        compiler_params=pltpu.CompilerParams(vmem_limit_bytes=24 << 20),
        name="border",
    )(where, in_hbm(corrected), in_hbm(atmosphere), up, dn, high, low)


def neighbours(low_part, high_part, axis):
    count = lax.axis_size(axis)
    forward = [(i, i + 1) for i in range(count - 1)]
    backward = [(b, a) for a, b in forward]
    return lax.ppermute(high_part, axis, forward), lax.ppermute(low_part, axis, backward)


def on_device(ifg_real, ifg_imag, date_pairs):
    n, rows, cols = ifg_real.shape
    rows_t, fwd, inv, back_up, back_dn = (jnp.asarray(t) for t in tables())
    col_t, row_t = blur_tables(rows * lax.axis_size("row"), rows, cols)
    own = row_t[:, :, RADIUS : RADIUS + rows]
    edges = np.stack([row_t[:, :RADIUS, :RADIUS], row_t[:, rows - RADIUS :, rows + RADIUS :]], axis=1)
    where = lax.axis_index("row").astype(jnp.int32).reshape(1)

    low = jnp.stack([ifg_real[:, :HALF], ifg_imag[:, :HALF]])
    high = jnp.stack([ifg_real[:, rows - HALF :], ifg_imag[:, rows - HALF :]])
    above, below = neighbours(low, high, "row")
    u = centre(ifg_real, ifg_imag, rows_t, fwd, inv)
    p, g = projection(date_pairs)
    series = ()
    for upper, halo, back in ((True, above, back_up), (False, below, back_dn)):
        q = edge(upper, ifg_real, ifg_imag, halo, u, rows_t, fwd, inv, back)
        sines = lax.all_to_all(q, "ifg", split_axis=0, concat_axis=0, tiled=True)
        series = (invert(sines.reshape(-1, cols), p, g, *series),)
    devices = lax.axis_size("ifg")
    series = lax.all_to_all(
        series[0].reshape(devices, -1, LANES), "ifg", split_axis=0, concat_axis=0, tiled=True
    )
    series, smooth, low, high = gather(series.reshape(-1, LANES), *halves(col_t), rows, cols)
    up, dn = neighbours(low, high, "row")
    corrected, atmosphere = inner(where, series, smooth, *halves(own))
    return tuple(border(where, corrected, atmosphere, up, dn, *halves(edges)))


def solution(mesh):
    placed = (P("ifg", "row", None), P("ifg", "row", None), P())
    return jax.shard_map(
        on_device,
        mesh=mesh,
        in_specs=placed,
        out_specs=(P("ifg", "row", None), P("ifg", "row", None)),
        check_vma=False,
    )
```

```python
import math

import jax
import jax.numpy as jnp
import ml_dtypes
import numpy as np
from jax import lax
from jax.experimental import pallas as pl
from jax.experimental.pallas import tpu as pltpu
from jax.sharding import PartitionSpec as P

PATCH = 64
HALF = PATCH // 2
NDATES = 320
ITERS = 3
RADIUS = 16
SIGMA = 5.0
THRESHOLD = 0.3
BAND = 5
LANES = 128
DATE_PAD = 384
BF16 = jnp.bfloat16
F32 = jnp.float32


def bf16(x):
    return np.asarray(x, np.float32).astype(ml_dtypes.bfloat16)


def tables():
    n = np.arange(PATCH)
    angle = (n[:, None] * n[None, :] % PATCH) * (2.0 * math.pi / PATCH)
    c = bf16(np.cos(angle) / 8.0).astype(np.float64)
    s = bf16(np.sin(angle) / 8.0).astype(np.float64)
    taper = np.sin(math.pi * (n + 0.5) / PATCH) ** 2
    two = np.eye(2)
    zero = np.zeros((PATCH, PATCH))

    rows_strip = np.block([[c, s], [-s, c]])
    c2, s2 = np.kron(two, c), np.kron(two, s)
    forward = np.block([[c2, -s2], [s2, c2]])
    t2 = np.concatenate([taper, taper])
    inverse = np.block([[c2 * t2, s2 * t2], [-s2 * t2, c2 * t2]])
    ct, st = c * taper[:, None], s * taper[:, None]
    back = []
    for centre_rows, edge_rows in ((slice(0, HALF), slice(HALF, PATCH)), (slice(HALF, PATCH), slice(0, HALF))):
        c1, s1, c2, s2 = ct[centre_rows], st[centre_rows], ct[edge_rows], st[edge_rows]
        back.append(np.block([[c1, -s1, c2, -s2], [s1, c1, s2, c2]]))
    return tuple(bf16(x) for x in (rows_strip, forward, inverse, *back))


def gauss(distance):
    return np.where(np.abs(distance) <= RADIUS, np.exp(-0.5 * (distance / SIGMA) ** 2), 0.0)


def blur_tables(rows, local_rows, cols):
    i = np.arange(cols)
    by_col = gauss(i[:, None] - i[None, :])
    by_col = by_col / by_col.sum(0, keepdims=True)
    out = np.arange(rows)[:, None]
    src = np.arange(-RADIUS, rows + RADIUS)[None, :]
    by_row = gauss(src - out) * ((src >= 0) & (src < rows))
    by_row = by_row / by_row.sum(1, keepdims=True)
    blocks = [
        by_row[a : a + local_rows, a : a + local_rows + 2 * RADIUS]
        for a in range(0, rows, local_rows)
    ]
    return by_col.astype(np.float32), np.stack(blocks).astype(np.float32)


def mm(a, b):
    return jnp.dot(a, b, preferred_element_type=F32)


def spectral(y_re, y_im, fwd, inv):
    count = y_re.shape[1] // LANES
    pieces = []
    for c in range(count):
        sl = slice(c * LANES, (c + 1) * LANES)
        pieces.append(jnp.concatenate([y_re[:, sl], y_im[:, sl]], axis=1))
    f0, g0 = fwd[...], inv[...]

    def shaped(z):
        re, im = z[:, :LANES], z[:, LANES:]
        scale = lax.rsqrt(lax.rsqrt(re * re + im * im + 1.0))
        return jnp.concatenate([(re * scale).astype(BF16), (im * scale).astype(BF16)], axis=1)

    lane = lax.broadcasted_iota(jnp.int32, (y_re.shape[0], LANES), 1)

    def moved(y):
        rolled = [pltpu.roll(y[:, c * LANES : (c + 1) * LANES], HALF, axis=1) for c in range(count)]
        zero = jnp.zeros_like(rolled[0])
        before, after = [zero] + rolled, rolled + [zero]
        return [jnp.where(lane < HALF, a, b) for a, b in zip(before, after)]

    even = [
        shaped(mm(jnp.concatenate([a, b], axis=1), f0)) for a, b in zip(moved(y_re), moved(y_im))
    ]
    def back(z):
        u = mm(z, g0)
        return [pltpu.roll(u[:, :LANES], LANES - HALF, axis=1), pltpu.roll(u[:, LANES:], LANES - HALF, axis=1)]

    turned = [back(z) for z in even]
    out_re, out_im = [], []
    for c in range(count):
        u = mm(shaped(mm(pieces[c], f0)), g0)
        for out, k in ((out_re, 0), (out_im, 1)):
            other = jnp.where(lane < LANES - HALF, turned[c][k], turned[c + 1][k])
            out.append((u[:, k * LANES : (k + 1) * LANES] + other).astype(BF16))
    return jnp.concatenate(out_re, axis=1), jnp.concatenate(out_im, axis=1)


def stacked_rows(table, strips):
    y = [mm(table, x).astype(BF16) for x in strips]
    y_re = jnp.concatenate([t[:PATCH] for t in y], axis=0)
    y_im = jnp.concatenate([t[PATCH:] for t in y], axis=0)
    return y_re, y_im


def centre_kernel(re_ref, im_ref, rows_ref, fwd_ref, inv_ref, *refs):
    u_ref = refs[-1]
    n = re_ref.shape[0]
    strips = [jnp.concatenate([re_ref[i], im_ref[i]], axis=0) for i in range(n)]
    y_re, y_im = stacked_rows(rows_ref[...], strips)
    u_re, u_im = spectral(y_re, y_im, fwd_ref, inv_ref)
    for i in range(n):
        sl = slice(i * PATCH, (i + 1) * PATCH)
        u_ref[i, :PATCH] = u_re[sl]
        u_ref[i, PATCH:] = u_im[sl]


BATCH = 8


def in_hbm(x):
    return pltpu.with_memory_space_constraint(x, pltpu.HBM)


def whole(a):
    return pl.BlockSpec(a.shape, lambda i: (0,) * a.ndim)


def centre(re, im, rows_t, fwd, inv, *after):
    n, rows, cols = re.shape
    g = BATCH
    block = pl.BlockSpec((g, rows, cols), lambda i: (i, 0, 0))
    return pl.pallas_call(
        centre_kernel,
        grid=(n // g,),
        in_specs=[block, block, whole(rows_t), whole(fwd), whole(inv),
                  *(pl.BlockSpec(memory_space=pl.ANY) for _ in after)],
        out_specs=pl.BlockSpec((g, 2 * rows, cols), lambda i: (i, 0, 0)),
        out_shape=pltpu.HBM((n, 2 * rows, cols), BF16),
        compiler_params=pltpu.CompilerParams(vmem_limit_bytes=24 << 20),
        cost_estimate=pl.CostEstimate(
            flops=n * 2 * 64 * 256 * 256 * 26, bytes_accessed=n * rows * cols * 8,
            transcendentals=n * 64 * 2304,
        ),
        name="centre",
    )(*(in_hbm(x) for x in (re, im, rows_t, fwd, inv)), *after)


def pack_kernel(re_ref, im_ref, *refs):
    out_ref = refs[-1]
    out_ref[0] = re_ref[...]
    out_ref[1] = im_ref[...]


def pack(re, im, side, first, count, *after):
    n, rows, cols = re.shape
    g = BATCH
    block = pl.BlockSpec((g, HALF, cols), lambda i: (first // g + i, side, 0))
    return pl.pallas_call(
        pack_kernel,
        grid=(count // g,),
        in_specs=[block, block, *(pl.BlockSpec(memory_space=pl.ANY) for _ in after)],
        out_specs=pl.BlockSpec((2, g, HALF, cols), lambda i: (0, i, 0, 0)),
        out_shape=jax.ShapeDtypeStruct((2, count, HALF, cols), BF16),
        compiler_params=pltpu.CompilerParams(vmem_limit_bytes=16 << 20),
        name="pack",
    )(in_hbm(re), in_hbm(im), *after)


GROUP = 16


def edge_kernel(upper, re_ref, im_ref, halo_ref, u_ref, rows_ref, fwd_ref, inv_ref, back_ref, *refs):
    q_ref, keep = refs[-2:]
    g = re_ref.shape[0]
    part = pl.program_id(0) % (GROUP // g)
    strips = []
    for i in range(g):
        own = [re_ref[i], im_ref[i]]
        other = [halo_ref[0, i], halo_ref[1, i]]
        first, second = (other, own) if upper else (own, other)
        strips.append(jnp.concatenate([first[0], second[0], first[1], second[1]], axis=0))
    y_re, y_im = stacked_rows(rows_ref[...], strips)
    u_re, u_im = spectral(y_re, y_im, fwd_ref, inv_ref)
    for i in range(g):
        sl = slice(i * PATCH, (i + 1) * PATCH)
        f = mm(back_ref[...], jnp.concatenate([u_ref[i], u_re[sl], u_im[sl]], axis=0))
        re, im = f[:HALF], f[HALF:]
        q = im * lax.rsqrt(re * re + im * im + 1.0)
        for c in range(keep.shape[0]):
            keep[c, pl.ds(part * g + i, HALF, stride=GROUP), :] = q[:, c * LANES : (c + 1) * LANES]

    @pl.when(part == GROUP // g - 1)
    def _():
        for t in range(keep.shape[0]):
            block = keep[t].astype(BF16)
            q_ref[:, :, t * LANES : (t + 1) * LANES] = block.reshape(HALF, GROUP, LANES)


def edge(upper, first, re, im, halo, u, rows_t, fwd, inv, back, *done):
    n, rows, cols = re.shape
    g = BATCH
    side = 0 if upper else 1
    at = first // g
    block = pl.BlockSpec((g, HALF, cols), lambda i: (at + i, side, 0))
    operands = [re, im, halo, u, rows_t, fwd, inv, back]
    return pl.pallas_call(
        lambda *refs: edge_kernel(upper, *refs),
        grid=(halo.shape[1] // g,),
        in_specs=[block, block,
                  pl.BlockSpec((2, g, HALF, cols), lambda i: (0, i, 0, 0)),
                  pl.BlockSpec((g, 2 * rows, cols), lambda i: (at + i, 0, 0)),
                  *(whole(x) for x in operands[4:]),
                  *(pl.BlockSpec(memory_space=pl.ANY) for _ in done)],
        out_specs=pl.BlockSpec((HALF, GROUP, cols), lambda i: (0, (first + i * g) // GROUP, 0)),
        out_shape=pltpu.HBM((HALF, n, cols), BF16),
        scratch_shapes=[pltpu.VMEM((cols // LANES, HALF * GROUP, LANES), F32)],
        input_output_aliases={len(operands): 0} if done else {},
        compiler_params=pltpu.CompilerParams(vmem_limit_bytes=24 << 20),
        cost_estimate=pl.CostEstimate(
            flops=halo.shape[1] * 2 * 64 * 256 * 256 * 30,
            bytes_accessed=halo.shape[1] * rows * cols * 7,
            transcendentals=halo.shape[1] * 64 * 2304,
        ),
        name="upper" if upper else "lower",
    )(*(x if x is halo else in_hbm(x) for x in operands), *(in_hbm(x) for x in done))


def projection_kernel(pairs_ref, pairs_t_ref, p_ref, g_ref, band, factor, solved):
    nifg = pairs_ref.shape[0]
    first, second = pairs_ref[:, 0:1], pairs_ref[:, 1:2]
    def design(width, wrap):
        dates = lax.broadcasted_iota(jnp.int32, (nifg, width), 1)
        if wrap:
            dates = jnp.where(dates >= NDATES, dates - NDATES, dates)
        return (jnp.where(dates == second, 1.0, 0.0) - jnp.where(dates == first, 1.0, 0.0)).astype(BF16)

    g_ref[...] = design(2 * NDATES, True)
    single = design(DATE_PAD, False)

    row_date = lax.broadcasted_iota(jnp.int32, (NDATES, nifg), 0)
    is_first = row_date == pairs_t_ref[0:1, :]
    is_either = is_first | (row_date == pairs_t_ref[1:2, :])
    first_t = jnp.where(is_first, 1.0, 0.0).astype(BF16)
    either_t = jnp.where(is_either, 1.0, 0.0).astype(BF16)
    gap = jnp.broadcast_to(second - first, (nifg, LANES))
    degree = mm(either_t, jnp.ones((nifg, LANES), BF16)) + 1.0
    band[...] = jnp.zeros_like(band)
    band[pl.ds(0, NDATES, stride=8), :] = degree
    for j in range(1, BAND + 1):
        match = jnp.where(gap == j, 1.0, 0.0).astype(BF16)
        band[pl.ds(j, NDATES, stride=8), :] = -mm(first_t, match)

    sub = lax.broadcasted_iota(jnp.int32, (8, LANES), 0)
    flat = sub * LANES + lax.broadcasted_iota(jnp.int32, (8, LANES), 1)

    def unit(i):
        return jnp.where(flat == i, 1.0, 0.0)

    def spread(x, j):
        return jnp.broadcast_to(x[j : j + 1, :], (8, LANES))

    def down(i, carry):
        rows, rhs = list(carry[: BAND + 1]), list(carry[BAND + 1 :])
        r, x = rows[0], rhs[0]
        inv = 1.0 / spread(r, 0)
        scaled = r * inv
        at = pl.ds(pl.multiple_of(i * 8, 8), 8)
        factor[at, :] = scaled
        solved[at, :] = x * inv
        for j in range(1, BAND + 1):
            moved = jnp.where(sub <= BAND - j, pltpu.roll(r, 8 - j, axis=0), 0.0)
            rows[j] = rows[j] - (spread(r, j) * moved) * inv
            rhs[j] = rhs[j] - spread(scaled, j) * x
        ahead = i + BAND + 1
        rows = rows[1:] + [band[pl.ds(pl.multiple_of(ahead * 8, 8), 8), :]]
        rhs = rhs[1:] + [unit(ahead)]
        return tuple(rows + rhs)

    start = [band[j * 8 : (j + 1) * 8, :] for j in range(BAND + 1)]
    start += [unit(j) for j in range(BAND + 1)]
    lax.fori_loop(0, NDATES, down, tuple(start), unroll=4)

    def up(t, carry):
        i = NDATES - 1 - t
        at = pl.ds(pl.multiple_of(i * 8, 8), 8)
        l = factor[at, :]
        x = solved[at, :]
        for j in range(BAND, 0, -1):
            x = x - spread(l, j) * carry[j - 1]
        solved[at, :] = x
        return (x,) + carry[:-1]

    zero = band[pl.ds((NDATES + BAND) * 8, 8), :]
    lax.fori_loop(0, NDATES, up, (zero,) * BAND, unroll=8)

    total = jnp.zeros((NDATES, nifg), F32)
    inverse = jnp.concatenate(
        [solved[pl.ds(c, NDATES, stride=8), :] for c in range(DATE_PAD // LANES)], axis=1
    )
    rest = inverse
    for _ in range(3):
        part = rest.astype(BF16)
        rest = rest - part.astype(F32)
        total = total + lax.dot_general(
            part, single, (((1,), (1,)), ((), ())), preferred_element_type=F32
        )
    high = total.astype(BF16)
    p_ref[...] = high


def projection(date_pairs):
    nifg = date_pairs.shape[0]
    tail = (NDATES + 2 * BAND + 6) * 8
    return pl.pallas_call(
        projection_kernel,
        out_shape=(
            pltpu.HBM((NDATES, nifg), BF16),
            pltpu.HBM((nifg, 2 * NDATES), BF16),
        ),
        scratch_shapes=[
            pltpu.VMEM((tail, LANES), F32),
            pltpu.VMEM((NDATES * 8, LANES), F32),
            pltpu.VMEM((NDATES * 8, LANES), F32),
        ],
        compiler_params=pltpu.CompilerParams(vmem_limit_bytes=40 << 20),
        cost_estimate=pl.CostEstimate(
            flops=20_000_000_000, bytes_accessed=4_000_000, transcendentals=0
        ),
        name="projection",
    )(date_pairs, date_pairs.T)


def invert_kernel(d_ref, p_ref, g_ref, *refs):
    chains = range(d_ref.shape[1] // CHAIN)
    scaled = [d_ref[:, k * CHAIN : (k + 1) * CHAIN].astype(F32) * (1.0 / THRESHOLD) for k in chains]
    series = [None for k in chains]
    misfit = scaled
    for step in range(ITERS):
        if step > 0:
            parts = []
            for k in chains:
                high = series[k].astype(BF16)
                low = (series[k] - high.astype(F32)).astype(BF16)
                parts.append(jnp.concatenate([high, low], axis=0))
            misfit = [scaled[k] - mm(g_ref[...], parts[k]) for k in chains]
        change = [mm(p_ref[...], jnp.clip(misfit[k], -1.0, 1.0).astype(BF16)) for k in chains]
        series = [change[k] if step == 0 else series[k] + change[k] for k in chains]
    series = jnp.concatenate(series, axis=1) * THRESHOLD
    tiles = series.shape[1] // LANES
    place = pl.program_id(0) * tiles
    if len(refs) == 1:
        (m_ref,) = refs
        for t in range(tiles):
            m_ref[pl.ds(place + t, NDATES, stride=4), :] = series[:, t * LANES : (t + 1) * LANES]
        return
    other_ref, m_ref, keep = refs
    for t in range(tiles):
        keep[pl.ds(4 + place + t, NDATES, stride=8), :] = series[:, t * LANES : (t + 1) * LANES]

    @pl.when(pl.program_id(0) == pl.num_programs(0) - 1)
    def _():
        for t in range(4):
            keep[pl.ds(t, NDATES, stride=8), :] = other_ref[pl.ds(t, NDATES, stride=4), :]
        m_ref[...] = keep[...].astype(BF16)


WIDTH = 512
CHAIN = 512


def invert(sines, p, g, *other):
    nifg, pixels = sines.shape
    width = WIDTH
    rows = NDATES * (8 if other else 4)
    return pl.pallas_call(
        invert_kernel,
        grid=(pixels // width,),
        in_specs=[
            pl.BlockSpec((nifg, width), lambda i: (0, i)),
            whole(p), whole(g), *(whole(x) for x in other)
        ],
        out_specs=pl.BlockSpec((rows, LANES), lambda i: (0, 0)),
        out_shape=jax.ShapeDtypeStruct((rows, LANES), BF16) if other else pltpu.HBM((rows, LANES), F32),
        scratch_shapes=[pltpu.VMEM((rows, LANES), F32)] if other else [],
        compiler_params=pltpu.CompilerParams(vmem_limit_bytes=32 << 20),
        cost_estimate=pl.CostEstimate(
            flops=pixels * nifg * NDATES * 14, bytes_accessed=6_000_000, transcendentals=0
        ),
        name="invert_rest" if other else "invert",
    )(sines, in_hbm(p), in_hbm(g), *(in_hbm(x) for x in other))


def halves(table):
    high = bf16(table)
    return jnp.asarray(high), jnp.asarray(bf16(table - high.astype(np.float32)))


def split2(x):
    high = x.astype(BF16)
    return high, (x - high.astype(F32)).astype(BF16)


def dot3(a, b):
    (ah, al), (bh, bl) = a, b
    return mm(ah, bh) + (mm(ah, bl) + mm(al, bh))


def gather_kernel(got_ref, ch_ref, cl_ref, series_ref, smooth_ref, low_ref, high_ref, wide):
    dates, rows, cols = series_ref.shape
    tiles = cols // LANES
    wide[...] = got_ref[...].astype(F32)
    for d in range(dates):
        halves = []
        for h in range(2):
            halves.append(
                jnp.concatenate(
                    [
                        wide[pl.ds(d * 8 + h * tiles + c, HALF, stride=dates * 8), :]
                        for c in range(tiles)
                    ],
                    axis=1,
                )
            )
        x = jnp.concatenate(halves, axis=0)
        series_ref[d] = x
        x = x.astype(BF16)
        smooth = mm(x, ch_ref[...]) + mm(x, cl_ref[...])
        smooth_ref[d] = smooth
        low_ref[d] = smooth[:RADIUS].astype(BF16)
        high_ref[d] = smooth[rows - RADIUS :].astype(BF16)


def gather(got, col_high, col_low, rows, cols):
    dates = got.shape[0] // 8 // HALF
    block = jax.ShapeDtypeStruct((dates, rows, cols), F32)
    border = jax.ShapeDtypeStruct((dates, RADIUS, cols), BF16)
    return pl.pallas_call(
        gather_kernel,
        out_shape=(block, block, border, border),
        scratch_shapes=[pltpu.VMEM(got.shape, F32)],
        compiler_params=pltpu.CompilerParams(vmem_limit_bytes=24 << 20),
        name="gather",
    )(got, col_high, col_low)


def inner_kernel(where_ref, series_ref, smooth_ref, high_ref, low_ref, corr_ref, atm_ref):
    table = (high_ref[0], low_ref[0])
    for d in range(series_ref.shape[0]):
        atm = dot3(table, split2(smooth_ref[d]))
        atm_ref[d] = atm
        corr_ref[d] = series_ref[d] - atm


def inner(where, series, smooth, high, low):
    dates, rows, cols = series.shape
    g = 5
    block = pl.BlockSpec((g, rows, cols), lambda i, w: (i, 0, 0))
    table = pl.BlockSpec((1,) + high.shape[1:], lambda i, w: (w[0], 0, 0))
    return pl.pallas_call(
        inner_kernel,
        grid_spec=pltpu.PrefetchScalarGridSpec(
            num_scalar_prefetch=1,
            grid=(dates // g,),
            in_specs=[block, block, table, table],
            out_specs=[block, block],
        ),
        out_shape=(pltpu.HBM((dates, rows, cols), F32),) * 2,
        compiler_params=pltpu.CompilerParams(vmem_limit_bytes=24 << 20),
        cost_estimate=pl.CostEstimate(
            flops=dates * rows * cols * 1024, bytes_accessed=dates * rows * cols * 16, transcendentals=0
        ),
        name="inner",
    )(where, series, smooth, high, low)


def border_kernel(where_ref, corr_in, atm_in, up_ref, dn_ref, high_ref, low_ref, corr_ref, atm_ref):
    def add(halo_ref):
        for d in range(corr_in.shape[0]):
            x = halo_ref[d]
            more = mm(high_ref[0, 0], x) + mm(low_ref[0, 0], x)
            atm_ref[d] = atm_in[d] + more
            corr_ref[d] = corr_in[d] - more

    @pl.when(pl.program_id(0) == 0)
    def _():
        add(up_ref)

    @pl.when(pl.program_id(0) == 1)
    def _():
        add(dn_ref)


def border(where, corrected, atmosphere, up, dn, high, low):
    dates, rows, cols = corrected.shape
    last = rows // RADIUS - 1
    block = pl.BlockSpec((dates, RADIUS, cols), lambda i, w: (0, i * last, 0))
    halo = pl.BlockSpec(up.shape, lambda i, w: (0, 0, 0))
    table = pl.BlockSpec((1, 1) + high.shape[2:], lambda i, w: (w[0], i, 0, 0))
    return pl.pallas_call(
        border_kernel,
        grid_spec=pltpu.PrefetchScalarGridSpec(
            num_scalar_prefetch=1,
            grid=(2,),
            in_specs=[block, block, halo, halo, table, table],
            out_specs=[block, block],
        ),
        out_shape=(pltpu.HBM((dates, rows, cols), F32),) * 2,
        input_output_aliases={1: 0, 2: 1},
        compiler_params=pltpu.CompilerParams(vmem_limit_bytes=24 << 20),
        name="border",
    )(where, in_hbm(corrected), in_hbm(atmosphere), up, dn, high, low)


def neighbours(low_part, high_part, axis):
    count = lax.axis_size(axis)
    forward = [(i, i + 1) for i in range(count - 1)]
    backward = [(b, a) for a, b in forward]
    return lax.ppermute(high_part, axis, forward), lax.ppermute(low_part, axis, backward)


def on_device(ifg_real, ifg_imag, date_pairs):
    n, rows, cols = ifg_real.shape
    rows_t, fwd, inv, back_up, back_dn = (jnp.asarray(t) for t in tables())
    col_t, row_t = blur_tables(rows * lax.axis_size("row"), rows, cols)
    own = row_t[:, :, RADIUS : RADIUS + rows]
    edges = np.stack([row_t[:, :RADIUS, :RADIUS], row_t[:, rows - RADIUS :, rows + RADIUS :]], axis=1)
    where = lax.axis_index("row").astype(jnp.int32).reshape(1)

    count = lax.axis_size("row")
    onward = [(i, i + 1) for i in range(count - 1)]
    back = [(b, a) for a, b in onward]
    packed = pack(ifg_real, ifg_imag, 1, 0, n // 2)
    above = [lax.ppermute(packed, "row", onward)]
    packed = pack(ifg_real, ifg_imag, 1, n // 2, n // 2, packed)
    above += [lax.ppermute(packed, "row", onward)]
    packed = pack(ifg_real, ifg_imag, 0, 0, n, packed)
    below = lax.ppermute(packed, "row", back)
    u = centre(ifg_real, ifg_imag, rows_t, fwd, inv, packed)
    p, g = projection(date_pairs)
    q = ()
    for k, halo in enumerate(above):
        q = (edge(True, k * (n // 2), ifg_real, ifg_imag, halo, u, rows_t, fwd, inv, back_up, *q),)
    lower = edge(False, 0, ifg_real, ifg_imag, below, u, rows_t, fwd, inv, back_dn)
    series = ()
    for part in (*q, lower):
        sines = lax.all_to_all(part, "ifg", split_axis=0, concat_axis=0, tiled=True)
        series = (invert(sines.reshape(-1, cols), p, g, *series),)
    devices = lax.axis_size("ifg")
    series = lax.all_to_all(
        series[0].reshape(devices, -1, LANES), "ifg", split_axis=0, concat_axis=0, tiled=True
    )
    series, smooth, low, high = gather(series.reshape(-1, LANES), *halves(col_t), rows, cols)
    up, dn = neighbours(low, high, "row")
    corrected, atmosphere = inner(where, series, smooth, *halves(own))
    return tuple(border(where, corrected, atmosphere, up, dn, *halves(edges)))


def solution(mesh):
    placed = (P("ifg", "row", None), P("ifg", "row", None), P())
    return jax.shard_map(
        on_device,
        mesh=mesh,
        in_specs=placed,
        out_specs=(P("ifg", "row", None), P("ifg", "row", None)),
        check_vma=False,
    )
```

```python
import math

import jax
import jax.numpy as jnp
import ml_dtypes
import numpy as np
from jax import lax
from jax.experimental import pallas as pl
from jax.experimental.pallas import tpu as pltpu
from jax.sharding import PartitionSpec as P

PATCH = 64
HALF = PATCH // 2
NDATES = 320
ITERS = 3
RADIUS = 16
SIGMA = 5.0
THRESHOLD = 0.3
BAND = 5
LANES = 128
DATE_PAD = 384
BF16 = jnp.bfloat16
F32 = jnp.float32


def bf16(x):
    return np.asarray(x, np.float32).astype(ml_dtypes.bfloat16)


def tables():
    n = np.arange(PATCH)
    angle = (n[:, None] * n[None, :] % PATCH) * (2.0 * math.pi / PATCH)
    c = bf16(np.cos(angle) / 8.0).astype(np.float64)
    s = bf16(np.sin(angle) / 8.0).astype(np.float64)
    taper = np.sin(math.pi * (n + 0.5) / PATCH) ** 2
    two = np.eye(2)
    zero = np.zeros((PATCH, PATCH))

    rows_strip = np.block([[c, s], [-s, c]])
    c2, s2 = np.kron(two, c), np.kron(two, s)
    forward = np.block([[c2, -s2], [s2, c2]])
    t2 = np.concatenate([taper, taper])
    inverse = np.block([[c2 * t2, s2 * t2], [-s2 * t2, c2 * t2]])
    ct, st = c * taper[:, None], s * taper[:, None]
    back = []
    for centre_rows, edge_rows in ((slice(0, HALF), slice(HALF, PATCH)), (slice(HALF, PATCH), slice(0, HALF))):
        c1, s1, c2, s2 = ct[centre_rows], st[centre_rows], ct[edge_rows], st[edge_rows]
        back.append(np.block([[c1, -s1, c2, -s2], [s1, c1, s2, c2]]))
    return tuple(bf16(x) for x in (rows_strip, forward, inverse, *back))


def gauss(distance):
    return np.where(np.abs(distance) <= RADIUS, np.exp(-0.5 * (distance / SIGMA) ** 2), 0.0)


def blur_tables(rows, local_rows, cols):
    i = np.arange(cols)
    by_col = gauss(i[:, None] - i[None, :])
    by_col = by_col / by_col.sum(0, keepdims=True)
    out = np.arange(rows)[:, None]
    src = np.arange(-RADIUS, rows + RADIUS)[None, :]
    by_row = gauss(src - out) * ((src >= 0) & (src < rows))
    by_row = by_row / by_row.sum(1, keepdims=True)
    blocks = [
        by_row[a : a + local_rows, a : a + local_rows + 2 * RADIUS]
        for a in range(0, rows, local_rows)
    ]
    return by_col.astype(np.float32), np.stack(blocks).astype(np.float32)


def mm(a, b):
    return jnp.dot(a, b, preferred_element_type=F32)


def spectral(y_re, y_im, fwd, inv):
    count = y_re.shape[1] // LANES
    pieces = []
    for c in range(count):
        sl = slice(c * LANES, (c + 1) * LANES)
        pieces.append(jnp.concatenate([y_re[:, sl], y_im[:, sl]], axis=1))
    f0, g0 = fwd[...], inv[...]

    def shaped(z):
        re, im = z[:, :LANES], z[:, LANES:]
        scale = lax.rsqrt(lax.rsqrt(re * re + im * im + 1.0))
        return jnp.concatenate([(re * scale).astype(BF16), (im * scale).astype(BF16)], axis=1)

    lane = lax.broadcasted_iota(jnp.int32, (y_re.shape[0], LANES), 1)

    def moved(y):
        rolled = [pltpu.roll(y[:, c * LANES : (c + 1) * LANES], HALF, axis=1) for c in range(count)]
        zero = jnp.zeros_like(rolled[0])
        before, after = [zero] + rolled, rolled + [zero]
        return [jnp.where(lane < HALF, a, b) for a, b in zip(before, after)]

    even = [
        shaped(mm(jnp.concatenate([a, b], axis=1), f0)) for a, b in zip(moved(y_re), moved(y_im))
    ]
    def back(z):
        u = mm(z, g0)
        return [pltpu.roll(u[:, :LANES], LANES - HALF, axis=1), pltpu.roll(u[:, LANES:], LANES - HALF, axis=1)]

    turned = [back(z) for z in even]
    out_re, out_im = [], []
    for c in range(count):
        u = mm(shaped(mm(pieces[c], f0)), g0)
        for out, k in ((out_re, 0), (out_im, 1)):
            other = jnp.where(lane < LANES - HALF, turned[c][k], turned[c + 1][k])
            out.append((u[:, k * LANES : (k + 1) * LANES] + other).astype(BF16))
    return jnp.concatenate(out_re, axis=1), jnp.concatenate(out_im, axis=1)


def stacked_rows(table, strips):
    y = [mm(table, x).astype(BF16) for x in strips]
    y_re = jnp.concatenate([t[:PATCH] for t in y], axis=0)
    y_im = jnp.concatenate([t[PATCH:] for t in y], axis=0)
    return y_re, y_im


def centre_kernel(re_ref, im_ref, rows_ref, fwd_ref, inv_ref, *refs):
    u_ref = refs[-1]
    n = re_ref.shape[0]
    strips = [jnp.concatenate([re_ref[i], im_ref[i]], axis=0) for i in range(n)]
    y_re, y_im = stacked_rows(rows_ref[...], strips)
    u_re, u_im = spectral(y_re, y_im, fwd_ref, inv_ref)
    for i in range(n):
        sl = slice(i * PATCH, (i + 1) * PATCH)
        u_ref[i, :PATCH] = u_re[sl]
        u_ref[i, PATCH:] = u_im[sl]


BATCH = 8


def in_hbm(x):
    return pltpu.with_memory_space_constraint(x, pltpu.HBM)


def whole(a):
    return pl.BlockSpec(a.shape, lambda i: (0,) * a.ndim)


def centre(re, im, rows_t, fwd, inv, *after):
    n, rows, cols = re.shape
    g = BATCH
    block = pl.BlockSpec((g, rows, cols), lambda i: (i, 0, 0))
    return pl.pallas_call(
        centre_kernel,
        grid=(n // g,),
        in_specs=[block, block, whole(rows_t), whole(fwd), whole(inv),
                  *(pl.BlockSpec(memory_space=pl.ANY) for _ in after)],
        out_specs=pl.BlockSpec((g, 2 * rows, cols), lambda i: (i, 0, 0)),
        out_shape=pltpu.HBM((n, 2 * rows, cols), BF16),
        compiler_params=pltpu.CompilerParams(vmem_limit_bytes=24 << 20),
        cost_estimate=pl.CostEstimate(
            flops=n * 2 * 64 * 256 * 256 * 26, bytes_accessed=n * rows * cols * 8,
            transcendentals=n * 64 * 2304,
        ),
        name="centre",
    )(*(in_hbm(x) for x in (re, im, rows_t, fwd, inv)), *after)


def pack_kernel(re_ref, im_ref, *out_refs):
    step, steps = pl.program_id(0), pl.num_programs(0)
    for part in range(2):

        @pl.when(step // (steps // 2) == part)
        def _():
            for side in range(2):
                out_ref = out_refs[2 * side + part]
                out_ref[0] = re_ref[:, side * HALF : (side + 1) * HALF]
                out_ref[1] = im_ref[:, side * HALF : (side + 1) * HALF]


def pack(re, im):
    n, rows, cols = re.shape
    g = BATCH
    steps = n // g
    block = pl.BlockSpec((g, rows, cols), lambda i: (i, 0, 0))
    early = pl.BlockSpec((2, g, HALF, cols), lambda i: (0, jnp.minimum(i, steps // 2 - 1), 0, 0))
    late = pl.BlockSpec((2, g, HALF, cols), lambda i: (0, jnp.maximum(i - steps // 2, 0), 0, 0))
    return pl.pallas_call(
        pack_kernel,
        grid=(steps,),
        in_specs=[block, block],
        out_specs=[early, late] * 2,
        out_shape=[jax.ShapeDtypeStruct((2, n // 2, HALF, cols), BF16)] * 4,
        compiler_params=pltpu.CompilerParams(vmem_limit_bytes=16 << 20),
        name="pack",
    )(in_hbm(re), in_hbm(im))


GROUP = 16


def edge_kernel(upper, re_ref, im_ref, halo_ref, u_ref, rows_ref, fwd_ref, inv_ref, back_ref, *refs):
    q_ref, keep = refs[-2:]
    g = re_ref.shape[0]
    part = pl.program_id(0) % (GROUP // g)
    strips = []
    for i in range(g):
        own = [re_ref[i], im_ref[i]]
        other = [halo_ref[0, i], halo_ref[1, i]]
        first, second = (other, own) if upper else (own, other)
        strips.append(jnp.concatenate([first[0], second[0], first[1], second[1]], axis=0))
    y_re, y_im = stacked_rows(rows_ref[...], strips)
    u_re, u_im = spectral(y_re, y_im, fwd_ref, inv_ref)
    for i in range(g):
        sl = slice(i * PATCH, (i + 1) * PATCH)
        f = mm(back_ref[...], jnp.concatenate([u_ref[i], u_re[sl], u_im[sl]], axis=0))
        re, im = f[:HALF], f[HALF:]
        q = im * lax.rsqrt(re * re + im * im + 1.0)
        for c in range(keep.shape[0]):
            keep[c, pl.ds(part * g + i, HALF, stride=GROUP), :] = q[:, c * LANES : (c + 1) * LANES]

    @pl.when(part == GROUP // g - 1)
    def _():
        for t in range(keep.shape[0]):
            block = keep[t].astype(BF16)
            q_ref[:, :, t * LANES : (t + 1) * LANES] = block.reshape(HALF, GROUP, LANES)


def edge(upper, first, re, im, halo, u, rows_t, fwd, inv, back, *done):
    n, rows, cols = re.shape
    g = BATCH
    side = 0 if upper else 1
    at = first // g
    block = pl.BlockSpec((g, HALF, cols), lambda i: (at + i, side, 0))
    operands = [re, im, halo, u, rows_t, fwd, inv, back]
    return pl.pallas_call(
        lambda *refs: edge_kernel(upper, *refs),
        grid=(halo.shape[1] // g,),
        in_specs=[block, block,
                  pl.BlockSpec((2, g, HALF, cols), lambda i: (0, i, 0, 0)),
                  pl.BlockSpec((g, 2 * rows, cols), lambda i: (at + i, 0, 0)),
                  *(whole(x) for x in operands[4:]),
                  *(pl.BlockSpec(memory_space=pl.ANY) for _ in done)],
        out_specs=pl.BlockSpec((HALF, GROUP, cols), lambda i: (0, (first + i * g) // GROUP, 0)),
        out_shape=pltpu.HBM((HALF, n, cols), BF16),
        scratch_shapes=[pltpu.VMEM((cols // LANES, HALF * GROUP, LANES), F32)],
        input_output_aliases={len(operands): 0} if done else {},
        compiler_params=pltpu.CompilerParams(vmem_limit_bytes=24 << 20),
        cost_estimate=pl.CostEstimate(
            flops=halo.shape[1] * 2 * 64 * 256 * 256 * 30,
            bytes_accessed=halo.shape[1] * rows * cols * 7,
            transcendentals=halo.shape[1] * 64 * 2304,
        ),
        name="upper" if upper else "lower",
    )(*(x if x is halo else in_hbm(x) for x in operands), *(in_hbm(x) for x in done))


def projection_kernel(pairs_ref, pairs_t_ref, p_ref, g_ref, band, factor, solved):
    nifg = pairs_ref.shape[0]
    first, second = pairs_ref[:, 0:1], pairs_ref[:, 1:2]
    def design(width, wrap):
        dates = lax.broadcasted_iota(jnp.int32, (nifg, width), 1)
        if wrap:
            dates = jnp.where(dates >= NDATES, dates - NDATES, dates)
        return (jnp.where(dates == second, 1.0, 0.0) - jnp.where(dates == first, 1.0, 0.0)).astype(BF16)

    g_ref[...] = design(2 * NDATES, True)
    single = design(DATE_PAD, False)

    row_date = lax.broadcasted_iota(jnp.int32, (NDATES, nifg), 0)
    is_first = row_date == pairs_t_ref[0:1, :]
    is_either = is_first | (row_date == pairs_t_ref[1:2, :])
    first_t = jnp.where(is_first, 1.0, 0.0).astype(BF16)
    either_t = jnp.where(is_either, 1.0, 0.0).astype(BF16)
    gap = jnp.broadcast_to(second - first, (nifg, LANES))
    degree = mm(either_t, jnp.ones((nifg, LANES), BF16)) + 1.0
    band[...] = jnp.zeros_like(band)
    band[pl.ds(0, NDATES, stride=8), :] = degree
    for j in range(1, BAND + 1):
        match = jnp.where(gap == j, 1.0, 0.0).astype(BF16)
        band[pl.ds(j, NDATES, stride=8), :] = -mm(first_t, match)

    sub = lax.broadcasted_iota(jnp.int32, (8, LANES), 0)
    flat = sub * LANES + lax.broadcasted_iota(jnp.int32, (8, LANES), 1)

    def unit(i):
        return jnp.where(flat == i, 1.0, 0.0)

    def spread(x, j):
        return jnp.broadcast_to(x[j : j + 1, :], (8, LANES))

    def down(i, carry):
        rows, rhs = list(carry[: BAND + 1]), list(carry[BAND + 1 :])
        r, x = rows[0], rhs[0]
        inv = 1.0 / spread(r, 0)
        scaled = r * inv
        at = pl.ds(pl.multiple_of(i * 8, 8), 8)
        factor[at, :] = scaled
        solved[at, :] = x * inv
        for j in range(1, BAND + 1):
            moved = jnp.where(sub <= BAND - j, pltpu.roll(r, 8 - j, axis=0), 0.0)
            rows[j] = rows[j] - (spread(r, j) * moved) * inv
            rhs[j] = rhs[j] - spread(scaled, j) * x
        ahead = i + BAND + 1
        rows = rows[1:] + [band[pl.ds(pl.multiple_of(ahead * 8, 8), 8), :]]
        rhs = rhs[1:] + [unit(ahead)]
        return tuple(rows + rhs)

    start = [band[j * 8 : (j + 1) * 8, :] for j in range(BAND + 1)]
    start += [unit(j) for j in range(BAND + 1)]
    lax.fori_loop(0, NDATES, down, tuple(start), unroll=4)

    def up(t, carry):
        i = NDATES - 1 - t
        at = pl.ds(pl.multiple_of(i * 8, 8), 8)
        l = factor[at, :]
        x = solved[at, :]
        for j in range(BAND, 0, -1):
            x = x - spread(l, j) * carry[j - 1]
        solved[at, :] = x
        return (x,) + carry[:-1]

    zero = band[pl.ds((NDATES + BAND) * 8, 8), :]
    lax.fori_loop(0, NDATES, up, (zero,) * BAND, unroll=8)

    total = jnp.zeros((NDATES, nifg), F32)
    inverse = jnp.concatenate(
        [solved[pl.ds(c, NDATES, stride=8), :] for c in range(DATE_PAD // LANES)], axis=1
    )
    rest = inverse
    for _ in range(3):
        part = rest.astype(BF16)
        rest = rest - part.astype(F32)
        total = total + lax.dot_general(
            part, single, (((1,), (1,)), ((), ())), preferred_element_type=F32
        )
    high = total.astype(BF16)
    p_ref[...] = high


def projection(date_pairs):
    nifg = date_pairs.shape[0]
    tail = (NDATES + 2 * BAND + 6) * 8
    return pl.pallas_call(
        projection_kernel,
        out_shape=(
            pltpu.HBM((NDATES, nifg), BF16),
            pltpu.HBM((nifg, 2 * NDATES), BF16),
        ),
        scratch_shapes=[
            pltpu.VMEM((tail, LANES), F32),
            pltpu.VMEM((NDATES * 8, LANES), F32),
            pltpu.VMEM((NDATES * 8, LANES), F32),
        ],
        compiler_params=pltpu.CompilerParams(vmem_limit_bytes=40 << 20),
        cost_estimate=pl.CostEstimate(
            flops=20_000_000_000, bytes_accessed=4_000_000, transcendentals=0
        ),
        name="projection",
    )(date_pairs, date_pairs.T)


def invert_kernel(d_ref, p_ref, g_ref, *refs):
    chains = range(d_ref.shape[1] // CHAIN)
    scaled = [d_ref[:, k * CHAIN : (k + 1) * CHAIN].astype(F32) * (1.0 / THRESHOLD) for k in chains]
    series = [None for k in chains]
    misfit = scaled
    for step in range(ITERS):
        if step > 0:
            parts = []
            for k in chains:
                high = series[k].astype(BF16)
                low = (series[k] - high.astype(F32)).astype(BF16)
                parts.append(jnp.concatenate([high, low], axis=0))
            misfit = [scaled[k] - mm(g_ref[...], parts[k]) for k in chains]
        change = [mm(p_ref[...], jnp.clip(misfit[k], -1.0, 1.0).astype(BF16)) for k in chains]
        series = [change[k] if step == 0 else series[k] + change[k] for k in chains]
    series = jnp.concatenate(series, axis=1) * THRESHOLD
    tiles = series.shape[1] // LANES
    place = pl.program_id(0) * tiles
    if len(refs) == 1:
        (m_ref,) = refs
        for t in range(tiles):
            m_ref[pl.ds(place + t, NDATES, stride=4), :] = series[:, t * LANES : (t + 1) * LANES]
        return
    other_ref, m_ref, keep = refs
    for t in range(tiles):
        keep[pl.ds(4 + place + t, NDATES, stride=8), :] = series[:, t * LANES : (t + 1) * LANES]

    @pl.when(pl.program_id(0) == pl.num_programs(0) - 1)
    def _():
        for t in range(4):
            keep[pl.ds(t, NDATES, stride=8), :] = other_ref[pl.ds(t, NDATES, stride=4), :]
        m_ref[...] = keep[...].astype(BF16)


WIDTH = 512
CHAIN = 512


def invert(sines, p, g, *other):
    nifg, pixels = sines.shape
    width = WIDTH
    rows = NDATES * (8 if other else 4)
    return pl.pallas_call(
        invert_kernel,
        grid=(pixels // width,),
        in_specs=[
            pl.BlockSpec((nifg, width), lambda i: (0, i)),
            whole(p), whole(g), *(whole(x) for x in other)
        ],
        out_specs=pl.BlockSpec((rows, LANES), lambda i: (0, 0)),
        out_shape=jax.ShapeDtypeStruct((rows, LANES), BF16) if other else pltpu.HBM((rows, LANES), F32),
        scratch_shapes=[pltpu.VMEM((rows, LANES), F32)] if other else [],
        compiler_params=pltpu.CompilerParams(vmem_limit_bytes=32 << 20),
        cost_estimate=pl.CostEstimate(
            flops=pixels * nifg * NDATES * 14, bytes_accessed=6_000_000, transcendentals=0
        ),
        name="invert_rest" if other else "invert",
    )(sines, in_hbm(p), in_hbm(g), *(in_hbm(x) for x in other))


def halves(table):
    high = bf16(table)
    return jnp.asarray(high), jnp.asarray(bf16(table - high.astype(np.float32)))


def split2(x):
    high = x.astype(BF16)
    return high, (x - high.astype(F32)).astype(BF16)


def dot3(a, b):
    (ah, al), (bh, bl) = a, b
    return mm(ah, bh) + (mm(ah, bl) + mm(al, bh))


def gather_kernel(got_ref, ch_ref, cl_ref, series_ref, smooth_ref, low_ref, high_ref, wide):
    dates, rows, cols = series_ref.shape
    tiles = cols // LANES
    wide[...] = got_ref[...].astype(F32)
    for d in range(dates):
        halves = []
        for h in range(2):
            halves.append(
                jnp.concatenate(
                    [
                        wide[pl.ds(d * 8 + h * tiles + c, HALF, stride=dates * 8), :]
                        for c in range(tiles)
                    ],
                    axis=1,
                )
            )
        x = jnp.concatenate(halves, axis=0)
        series_ref[d] = x
        x = x.astype(BF16)
        smooth = mm(x, ch_ref[...]) + mm(x, cl_ref[...])
        smooth_ref[d] = smooth
        low_ref[d] = smooth[:RADIUS].astype(BF16)
        high_ref[d] = smooth[rows - RADIUS :].astype(BF16)


def gather(got, col_high, col_low, rows, cols):
    dates = got.shape[0] // 8 // HALF
    block = jax.ShapeDtypeStruct((dates, rows, cols), F32)
    border = jax.ShapeDtypeStruct((dates, RADIUS, cols), BF16)
    return pl.pallas_call(
        gather_kernel,
        out_shape=(block, block, border, border),
        scratch_shapes=[pltpu.VMEM(got.shape, F32)],
        compiler_params=pltpu.CompilerParams(vmem_limit_bytes=24 << 20),
        name="gather",
    )(got, col_high, col_low)


def inner_kernel(where_ref, series_ref, smooth_ref, high_ref, low_ref, corr_ref, atm_ref):
    table = (high_ref[0], low_ref[0])
    for d in range(series_ref.shape[0]):
        atm = dot3(table, split2(smooth_ref[d]))
        atm_ref[d] = atm
        corr_ref[d] = series_ref[d] - atm


def inner(where, series, smooth, high, low):
    dates, rows, cols = series.shape
    g = 5
    block = pl.BlockSpec((g, rows, cols), lambda i, w: (i, 0, 0))
    table = pl.BlockSpec((1,) + high.shape[1:], lambda i, w: (w[0], 0, 0))
    return pl.pallas_call(
        inner_kernel,
        grid_spec=pltpu.PrefetchScalarGridSpec(
            num_scalar_prefetch=1,
            grid=(dates // g,),
            in_specs=[block, block, table, table],
            out_specs=[block, block],
        ),
        out_shape=(pltpu.HBM((dates, rows, cols), F32),) * 2,
        compiler_params=pltpu.CompilerParams(vmem_limit_bytes=24 << 20),
        cost_estimate=pl.CostEstimate(
            flops=dates * rows * cols * 1024, bytes_accessed=dates * rows * cols * 16, transcendentals=0
        ),
        name="inner",
    )(where, series, smooth, high, low)


def border_kernel(where_ref, corr_in, atm_in, up_ref, dn_ref, high_ref, low_ref, corr_ref, atm_ref):
    def add(halo_ref):
        for d in range(corr_in.shape[0]):
            x = halo_ref[d]
            more = mm(high_ref[0, 0], x) + mm(low_ref[0, 0], x)
            atm_ref[d] = atm_in[d] + more
            corr_ref[d] = corr_in[d] - more

    @pl.when(pl.program_id(0) == 0)
    def _():
        add(up_ref)

    @pl.when(pl.program_id(0) == 1)
    def _():
        add(dn_ref)


def border(where, corrected, atmosphere, up, dn, high, low):
    dates, rows, cols = corrected.shape
    last = rows // RADIUS - 1
    block = pl.BlockSpec((dates, RADIUS, cols), lambda i, w: (0, i * last, 0))
    halo = pl.BlockSpec(up.shape, lambda i, w: (0, 0, 0))
    table = pl.BlockSpec((1, 1) + high.shape[2:], lambda i, w: (w[0], i, 0, 0))
    return pl.pallas_call(
        border_kernel,
        grid_spec=pltpu.PrefetchScalarGridSpec(
            num_scalar_prefetch=1,
            grid=(2,),
            in_specs=[block, block, halo, halo, table, table],
            out_specs=[block, block],
        ),
        out_shape=(pltpu.HBM((dates, rows, cols), F32),) * 2,
        input_output_aliases={1: 0, 2: 1},
        compiler_params=pltpu.CompilerParams(vmem_limit_bytes=24 << 20),
        name="border",
    )(where, in_hbm(corrected), in_hbm(atmosphere), up, dn, high, low)


def neighbours(low_part, high_part, axis):
    count = lax.axis_size(axis)
    forward = [(i, i + 1) for i in range(count - 1)]
    backward = [(b, a) for a, b in forward]
    return lax.ppermute(high_part, axis, forward), lax.ppermute(low_part, axis, backward)


def on_device(ifg_real, ifg_imag, date_pairs):
    n, rows, cols = ifg_real.shape
    rows_t, fwd, inv, back_up, back_dn = (jnp.asarray(t) for t in tables())
    col_t, row_t = blur_tables(rows * lax.axis_size("row"), rows, cols)
    own = row_t[:, :, RADIUS : RADIUS + rows]
    edges = np.stack([row_t[:, :RADIUS, :RADIUS], row_t[:, rows - RADIUS :, rows + RADIUS :]], axis=1)
    where = lax.axis_index("row").astype(jnp.int32).reshape(1)

    count = lax.axis_size("row")
    onward = [(i, i + 1) for i in range(count - 1)]
    back = [(b, a) for a, b in onward]
    packed = pack(ifg_real, ifg_imag)
    above = [lax.ppermute(part, "row", onward) for part in packed[2:]]
    below = [lax.ppermute(part, "row", back) for part in packed[:2]]
    u = centre(ifg_real, ifg_imag, rows_t, fwd, inv, packed[2])
    p, g = projection(date_pairs)
    sides = []
    for upper, parts, table in ((True, above, back_up), (False, below, back_dn)):
        q = ()
        for k, halo in enumerate(parts):
            q = (edge(upper, k * (n // 2), ifg_real, ifg_imag, halo, u, rows_t, fwd, inv, table, *q),)
        sides += q
    series = ()
    for part in sides:
        sines = lax.all_to_all(part, "ifg", split_axis=0, concat_axis=0, tiled=True)
        series = (invert(sines.reshape(-1, cols), p, g, *series),)
    devices = lax.axis_size("ifg")
    series = lax.all_to_all(
        series[0].reshape(devices, -1, LANES), "ifg", split_axis=0, concat_axis=0, tiled=True
    )
    series, smooth, low, high = gather(series.reshape(-1, LANES), *halves(col_t), rows, cols)
    up, dn = neighbours(low, high, "row")
    corrected, atmosphere = inner(where, series, smooth, *halves(own))
    return tuple(border(where, corrected, atmosphere, up, dn, *halves(edges)))


def solution(mesh):
    placed = (P("ifg", "row", None), P("ifg", "row", None), P())
    return jax.shard_map(
        on_device,
        mesh=mesh,
        in_specs=placed,
        out_specs=(P("ifg", "row", None), P("ifg", "row", None)),
        check_vma=False,
    )
```

```python
import math

import jax
import jax.numpy as jnp
import ml_dtypes
import numpy as np
from jax import lax
from jax.experimental import pallas as pl
from jax.experimental.pallas import tpu as pltpu
from jax.sharding import PartitionSpec as P

PATCH = 64
HALF = PATCH // 2
NDATES = 320
ITERS = 3
RADIUS = 16
SIGMA = 5.0
THRESHOLD = 0.3
BAND = 5
LANES = 128
DATE_PAD = 384
BF16 = jnp.bfloat16
F32 = jnp.float32


def bf16(x):
    return np.asarray(x, np.float32).astype(ml_dtypes.bfloat16)


def tables():
    n = np.arange(PATCH)
    angle = (n[:, None] * n[None, :] % PATCH) * (2.0 * math.pi / PATCH)
    c = bf16(np.cos(angle) / 8.0).astype(np.float64)
    s = bf16(np.sin(angle) / 8.0).astype(np.float64)
    taper = np.sin(math.pi * (n + 0.5) / PATCH) ** 2
    two = np.eye(2)
    zero = np.zeros((PATCH, PATCH))

    rows_strip = np.block([[c, s], [-s, c]])
    c2, s2 = np.kron(two, c), np.kron(two, s)
    forward = np.block([[c2, -s2], [s2, c2]])
    t2 = np.concatenate([taper, taper])
    inverse = np.block([[c2 * t2, s2 * t2], [-s2 * t2, c2 * t2]])
    ct, st = c * taper[:, None], s * taper[:, None]
    back = []
    for centre_rows, edge_rows in ((slice(0, HALF), slice(HALF, PATCH)), (slice(HALF, PATCH), slice(0, HALF))):
        c1, s1, c2, s2 = ct[centre_rows], st[centre_rows], ct[edge_rows], st[edge_rows]
        back.append(np.block([[c1, -s1, c2, -s2], [s1, c1, s2, c2]]))
    return tuple(bf16(x) for x in (rows_strip, forward, inverse, *back))


def gauss(distance):
    return np.where(np.abs(distance) <= RADIUS, np.exp(-0.5 * (distance / SIGMA) ** 2), 0.0)


def blur_tables(rows, local_rows, cols):
    i = np.arange(cols)
    by_col = gauss(i[:, None] - i[None, :])
    by_col = by_col / by_col.sum(0, keepdims=True)
    out = np.arange(rows)[:, None]
    src = np.arange(-RADIUS, rows + RADIUS)[None, :]
    by_row = gauss(src - out) * ((src >= 0) & (src < rows))
    by_row = by_row / by_row.sum(1, keepdims=True)
    blocks = [
        by_row[a : a + local_rows, a : a + local_rows + 2 * RADIUS]
        for a in range(0, rows, local_rows)
    ]
    return by_col.astype(np.float32), np.stack(blocks).astype(np.float32)


def mm(a, b):
    return jnp.dot(a, b, preferred_element_type=F32)


def spectral(y_re, y_im, fwd, inv):
    count = y_re.shape[1] // LANES
    pieces = []
    for c in range(count):
        sl = slice(c * LANES, (c + 1) * LANES)
        pieces.append(jnp.concatenate([y_re[:, sl], y_im[:, sl]], axis=1))
    f0, g0 = fwd[...], inv[...]

    def shaped(z):
        re, im = z[:, :LANES], z[:, LANES:]
        scale = lax.rsqrt(lax.rsqrt(re * re + im * im + 1.0))
        return jnp.concatenate([(re * scale).astype(BF16), (im * scale).astype(BF16)], axis=1)

    lane = lax.broadcasted_iota(jnp.int32, (y_re.shape[0], LANES), 1)

    def moved(y):
        rolled = [pltpu.roll(y[:, c * LANES : (c + 1) * LANES], HALF, axis=1) for c in range(count)]
        zero = jnp.zeros_like(rolled[0])
        before, after = [zero] + rolled, rolled + [zero]
        return [jnp.where(lane < HALF, a, b) for a, b in zip(before, after)]

    even = [
        shaped(mm(jnp.concatenate([a, b], axis=1), f0)) for a, b in zip(moved(y_re), moved(y_im))
    ]
    def back(z):
        u = mm(z, g0)
        return [pltpu.roll(u[:, :LANES], LANES - HALF, axis=1), pltpu.roll(u[:, LANES:], LANES - HALF, axis=1)]

    turned = [back(z) for z in even]
    out_re, out_im = [], []
    for c in range(count):
        u = mm(shaped(mm(pieces[c], f0)), g0)
        for out, k in ((out_re, 0), (out_im, 1)):
            other = jnp.where(lane < LANES - HALF, turned[c][k], turned[c + 1][k])
            out.append((u[:, k * LANES : (k + 1) * LANES] + other).astype(BF16))
    return jnp.concatenate(out_re, axis=1), jnp.concatenate(out_im, axis=1)


def stacked_rows(table, strips):
    y = [mm(table, x).astype(BF16) for x in strips]
    y_re = jnp.concatenate([t[:PATCH] for t in y], axis=0)
    y_im = jnp.concatenate([t[PATCH:] for t in y], axis=0)
    return y_re, y_im


def centre_kernel(re_ref, im_ref, rows_ref, fwd_ref, inv_ref, u_ref):
    n = re_ref.shape[0]
    strips = [jnp.concatenate([re_ref[i], im_ref[i]], axis=0) for i in range(n)]
    y_re, y_im = stacked_rows(rows_ref[...], strips)
    u_re, u_im = spectral(y_re, y_im, fwd_ref, inv_ref)
    for i in range(n):
        sl = slice(i * PATCH, (i + 1) * PATCH)
        u_ref[i, :PATCH] = u_re[sl]
        u_ref[i, PATCH:] = u_im[sl]


BATCH = 8


def in_hbm(x):
    return pltpu.with_memory_space_constraint(x, pltpu.HBM)


def whole(a):
    return pl.BlockSpec(a.shape, lambda i: (0,) * a.ndim)


def centre(re, im, rows_t, fwd, inv):
    n, rows, cols = re.shape
    g = BATCH
    block = pl.BlockSpec((g, rows, cols), lambda i: (i, 0, 0))
    return pl.pallas_call(
        centre_kernel,
        grid=(n // g,),
        in_specs=[block, block, whole(rows_t), whole(fwd), whole(inv)],
        out_specs=pl.BlockSpec((g, 2 * rows, cols), lambda i: (i, 0, 0)),
        out_shape=pltpu.HBM((n, 2 * rows, cols), BF16),
        compiler_params=pltpu.CompilerParams(vmem_limit_bytes=24 << 20),
        cost_estimate=pl.CostEstimate(
            flops=n * 2 * 64 * 256 * 256 * 26, bytes_accessed=n * rows * cols * 8,
            transcendentals=n * 64 * 2304,
        ),
        name="centre",
    )(*(in_hbm(x) for x in (re, im, rows_t, fwd, inv)))


GROUP = 16


def edge_kernel(upper, re_ref, im_ref, halo_ref, u_ref, rows_ref, fwd_ref, inv_ref, back_ref, q_ref, keep):
    g = re_ref.shape[0]
    part = pl.program_id(0) % (GROUP // g)
    strips = []
    for i in range(g):
        own = [re_ref[i], im_ref[i]]
        other = [halo_ref[0, i], halo_ref[1, i]]
        first, second = (other, own) if upper else (own, other)
        strips.append(jnp.concatenate([first[0], second[0], first[1], second[1]], axis=0))
    y_re, y_im = stacked_rows(rows_ref[...], strips)
    u_re, u_im = spectral(y_re, y_im, fwd_ref, inv_ref)
    for i in range(g):
        sl = slice(i * PATCH, (i + 1) * PATCH)
        f = mm(back_ref[...], jnp.concatenate([u_ref[i], u_re[sl], u_im[sl]], axis=0))
        re, im = f[:HALF], f[HALF:]
        q = im * lax.rsqrt(re * re + im * im + 1.0)
        for c in range(keep.shape[0]):
            keep[c, pl.ds(part * g + i, HALF, stride=GROUP), :] = q[:, c * LANES : (c + 1) * LANES]

    @pl.when(part == GROUP // g - 1)
    def _():
        for t in range(keep.shape[0]):
            block = keep[t].astype(BF16)
            q_ref[:, :, t * LANES : (t + 1) * LANES] = block.reshape(HALF, GROUP, LANES)


def edge(upper, re, im, halo, u, rows_t, fwd, inv, back):
    n, rows, cols = re.shape
    g = BATCH
    side = 0 if upper else 1
    block = pl.BlockSpec((g, HALF, cols), lambda i: (i, side, 0))
    return pl.pallas_call(
        lambda *refs: edge_kernel(upper, *refs),
        grid=(n // g,),
        in_specs=[block, block,
                  pl.BlockSpec((2, g, HALF, cols), lambda i: (0, i, 0, 0)),
                  pl.BlockSpec((g, 2 * rows, cols), lambda i: (i, 0, 0)),
                  whole(rows_t), whole(fwd), whole(inv), whole(back)],
        out_specs=pl.BlockSpec((HALF, GROUP, cols), lambda i: (0, i // (GROUP // g), 0)),
        out_shape=pltpu.HBM((HALF, n, cols), BF16),
        scratch_shapes=[pltpu.VMEM((cols // LANES, HALF * GROUP, LANES), F32)],
        compiler_params=pltpu.CompilerParams(vmem_limit_bytes=24 << 20),
        cost_estimate=pl.CostEstimate(
            flops=n * 2 * 64 * 256 * 256 * 30, bytes_accessed=n * rows * cols * 7,
            transcendentals=n * 64 * 2304,
        ),
        name="upper" if upper else "lower",
    )(in_hbm(re), in_hbm(im), halo, *(in_hbm(x) for x in (u, rows_t, fwd, inv, back)))


def projection_kernel(pairs_ref, pairs_t_ref, p_ref, g_ref, band, factor, solved):
    nifg = pairs_ref.shape[0]
    first, second = pairs_ref[:, 0:1], pairs_ref[:, 1:2]
    def design(width, wrap):
        dates = lax.broadcasted_iota(jnp.int32, (nifg, width), 1)
        if wrap:
            dates = jnp.where(dates >= NDATES, dates - NDATES, dates)
        return (jnp.where(dates == second, 1.0, 0.0) - jnp.where(dates == first, 1.0, 0.0)).astype(BF16)

    g_ref[...] = design(2 * NDATES, True)
    single = design(DATE_PAD, False)

    row_date = lax.broadcasted_iota(jnp.int32, (NDATES, nifg), 0)
    is_first = row_date == pairs_t_ref[0:1, :]
    is_either = is_first | (row_date == pairs_t_ref[1:2, :])
    first_t = jnp.where(is_first, 1.0, 0.0).astype(BF16)
    either_t = jnp.where(is_either, 1.0, 0.0).astype(BF16)
    gap = jnp.broadcast_to(second - first, (nifg, LANES))
    degree = mm(either_t, jnp.ones((nifg, LANES), BF16)) + 1.0
    band[...] = jnp.zeros_like(band)
    band[pl.ds(0, NDATES, stride=8), :] = degree
    for j in range(1, BAND + 1):
        match = jnp.where(gap == j, 1.0, 0.0).astype(BF16)
        band[pl.ds(j, NDATES, stride=8), :] = -mm(first_t, match)

    sub = lax.broadcasted_iota(jnp.int32, (8, LANES), 0)
    flat = sub * LANES + lax.broadcasted_iota(jnp.int32, (8, LANES), 1)

    def unit(i):
        return jnp.where(flat == i, 1.0, 0.0)

    def spread(x, j):
        return jnp.broadcast_to(x[j : j + 1, :], (8, LANES))

    def down(i, carry):
        rows, rhs = list(carry[: BAND + 1]), list(carry[BAND + 1 :])
        r, x = rows[0], rhs[0]
        inv = 1.0 / spread(r, 0)
        scaled = r * inv
        at = pl.ds(pl.multiple_of(i * 8, 8), 8)
        factor[at, :] = scaled
        solved[at, :] = x * inv
        for j in range(1, BAND + 1):
            moved = jnp.where(sub <= BAND - j, pltpu.roll(r, 8 - j, axis=0), 0.0)
            rows[j] = rows[j] - (spread(r, j) * moved) * inv
            rhs[j] = rhs[j] - spread(scaled, j) * x
        ahead = i + BAND + 1
        rows = rows[1:] + [band[pl.ds(pl.multiple_of(ahead * 8, 8), 8), :]]
        rhs = rhs[1:] + [unit(ahead)]
        return tuple(rows + rhs)

    start = [band[j * 8 : (j + 1) * 8, :] for j in range(BAND + 1)]
    start += [unit(j) for j in range(BAND + 1)]
    lax.fori_loop(0, NDATES, down, tuple(start), unroll=4)

    def up(t, carry):
        i = NDATES - 1 - t
        at = pl.ds(pl.multiple_of(i * 8, 8), 8)
        l = factor[at, :]
        x = solved[at, :]
        for j in range(BAND, 0, -1):
            x = x - spread(l, j) * carry[j - 1]
        solved[at, :] = x
        return (x,) + carry[:-1]

    zero = band[pl.ds((NDATES + BAND) * 8, 8), :]
    lax.fori_loop(0, NDATES, up, (zero,) * BAND, unroll=8)

    total = jnp.zeros((NDATES, nifg), F32)
    inverse = jnp.concatenate(
        [solved[pl.ds(c, NDATES, stride=8), :] for c in range(DATE_PAD // LANES)], axis=1
    )
    rest = inverse
    for _ in range(3):
        part = rest.astype(BF16)
        rest = rest - part.astype(F32)
        total = total + lax.dot_general(
            part, single, (((1,), (1,)), ((), ())), preferred_element_type=F32
        )
    high = total.astype(BF16)
    p_ref[...] = high


def projection(date_pairs):
    nifg = date_pairs.shape[0]
    tail = (NDATES + 2 * BAND + 6) * 8
    return pl.pallas_call(
        projection_kernel,
        out_shape=(
            pltpu.HBM((NDATES, nifg), BF16),
            pltpu.HBM((nifg, 2 * NDATES), BF16),
        ),
        scratch_shapes=[
            pltpu.VMEM((tail, LANES), F32),
            pltpu.VMEM((NDATES * 8, LANES), F32),
            pltpu.VMEM((NDATES * 8, LANES), F32),
        ],
        compiler_params=pltpu.CompilerParams(vmem_limit_bytes=40 << 20),
        cost_estimate=pl.CostEstimate(
            flops=20_000_000_000, bytes_accessed=4_000_000, transcendentals=0
        ),
        name="projection",
    )(date_pairs, date_pairs.T)


def invert_kernel(d_ref, p_ref, g_ref, *refs):
    chains = range(d_ref.shape[1] // CHAIN)
    scaled = [d_ref[:, k * CHAIN : (k + 1) * CHAIN].astype(F32) * (1.0 / THRESHOLD) for k in chains]
    series = [None for k in chains]
    misfit = scaled
    for step in range(ITERS):
        if step > 0:
            parts = []
            for k in chains:
                high = series[k].astype(BF16)
                low = (series[k] - high.astype(F32)).astype(BF16)
                parts.append(jnp.concatenate([high, low], axis=0))
            misfit = [scaled[k] - mm(g_ref[...], parts[k]) for k in chains]
        change = [mm(p_ref[...], jnp.clip(misfit[k], -1.0, 1.0).astype(BF16)) for k in chains]
        series = [change[k] if step == 0 else series[k] + change[k] for k in chains]
    series = jnp.concatenate(series, axis=1) * THRESHOLD
    tiles = series.shape[1] // LANES
    place = pl.program_id(0) * tiles
    if len(refs) == 1:
        (m_ref,) = refs
        for t in range(tiles):
            m_ref[pl.ds(place + t, NDATES, stride=4), :] = series[:, t * LANES : (t + 1) * LANES]
        return
    other_ref, m_ref, keep = refs
    for t in range(tiles):
        keep[pl.ds(4 + place + t, NDATES, stride=8), :] = series[:, t * LANES : (t + 1) * LANES]

    @pl.when(pl.program_id(0) == pl.num_programs(0) - 1)
    def _():
        for t in range(4):
            keep[pl.ds(t, NDATES, stride=8), :] = other_ref[pl.ds(t, NDATES, stride=4), :]
        m_ref[...] = keep[...].astype(BF16)


WIDTH = 512
CHAIN = 512


def invert(sines, p, g, *other):
    nifg, pixels = sines.shape
    width = WIDTH
    rows = NDATES * (8 if other else 4)
    return pl.pallas_call(
        invert_kernel,
        grid=(pixels // width,),
        in_specs=[
            pl.BlockSpec((nifg, width), lambda i: (0, i)),
            whole(p), whole(g), *(whole(x) for x in other)
        ],
        out_specs=pl.BlockSpec((rows, LANES), lambda i: (0, 0)),
        out_shape=jax.ShapeDtypeStruct((rows, LANES), BF16) if other else pltpu.HBM((rows, LANES), F32),
        scratch_shapes=[pltpu.VMEM((rows, LANES), F32)] if other else [],
        compiler_params=pltpu.CompilerParams(vmem_limit_bytes=32 << 20),
        cost_estimate=pl.CostEstimate(
            flops=pixels * nifg * NDATES * 14, bytes_accessed=6_000_000, transcendentals=0
        ),
        name="invert_rest" if other else "invert",
    )(sines, in_hbm(p), in_hbm(g), *(in_hbm(x) for x in other))


def halves(table):
    high = bf16(table)
    return jnp.asarray(high), jnp.asarray(bf16(table - high.astype(np.float32)))


def split2(x):
    high = x.astype(BF16)
    return high, (x - high.astype(F32)).astype(BF16)


def dot3(a, b):
    (ah, al), (bh, bl) = a, b
    return mm(ah, bh) + (mm(ah, bl) + mm(al, bh))


def gather_kernel(got_ref, ch_ref, cl_ref, series_ref, smooth_ref, low_ref, high_ref, wide):
    dates, rows, cols = series_ref.shape
    tiles = cols // LANES
    wide[...] = got_ref[...].astype(F32)
    for d in range(dates):
        halves = []
        for h in range(2):
            halves.append(
                jnp.concatenate(
                    [
                        wide[pl.ds(d * 8 + h * tiles + c, HALF, stride=dates * 8), :]
                        for c in range(tiles)
                    ],
                    axis=1,
                )
            )
        x = jnp.concatenate(halves, axis=0)
        series_ref[d] = x
        x = x.astype(BF16)
        smooth = mm(x, ch_ref[...]) + mm(x, cl_ref[...])
        smooth_ref[d] = smooth
        low_ref[d] = smooth[:RADIUS].astype(BF16)
        high_ref[d] = smooth[rows - RADIUS :].astype(BF16)


def gather(got, col_high, col_low, rows, cols):
    dates = got.shape[0] // 8 // HALF
    block = jax.ShapeDtypeStruct((dates, rows, cols), F32)
    border = jax.ShapeDtypeStruct((dates, RADIUS, cols), BF16)
    return pl.pallas_call(
        gather_kernel,
        out_shape=(block, block, border, border),
        scratch_shapes=[pltpu.VMEM(got.shape, F32)],
        compiler_params=pltpu.CompilerParams(vmem_limit_bytes=24 << 20),
        name="gather",
    )(got, col_high, col_low)


def finish_kernel(where_ref, series_ref, smooth_ref, up_ref, dn_ref, high_ref, low_ref, corr_ref, atm_ref):
    table = (high_ref[0], low_ref[0])
    for d in range(series_ref.shape[0]):
        smooth, rest = split2(smooth_ref[d])
        x = jnp.concatenate([up_ref[d], smooth, dn_ref[d]], axis=0)
        atm = mm(table[0], x) + (mm(table[1], x) + mm(table[0][:, RADIUS:-RADIUS], rest))
        atm_ref[d] = atm
        corr_ref[d] = series_ref[d] - atm


def finish(where, series, smooth, up, dn, high, low):
    dates, rows, cols = series.shape
    g = FINISH
    block = pl.BlockSpec((g, rows, cols), lambda i, w: (i, 0, 0))
    halo = pl.BlockSpec((g, RADIUS, cols), lambda i, w: (i, 0, 0))
    table = pl.BlockSpec((1,) + high.shape[1:], lambda i, w: (w[0], 0, 0))
    return pl.pallas_call(
        finish_kernel,
        grid_spec=pltpu.PrefetchScalarGridSpec(
            num_scalar_prefetch=1,
            grid=(dates // g,),
            in_specs=[block, block, halo, halo, table, table],
            out_specs=[block, block],
        ),
        out_shape=(jax.ShapeDtypeStruct((dates, rows, cols), F32),) * 2,
        compiler_params=pltpu.CompilerParams(vmem_limit_bytes=24 << 20),
        name="finish",
    )(where, series, smooth, up, dn, high, low)


FINISH = 5


def neighbours(low_part, high_part, axis):
    count = lax.axis_size(axis)
    forward = [(i, i + 1) for i in range(count - 1)]
    backward = [(b, a) for a, b in forward]
    return lax.ppermute(high_part, axis, forward), lax.ppermute(low_part, axis, backward)


def on_device(ifg_real, ifg_imag, date_pairs):
    n, rows, cols = ifg_real.shape
    rows_t, fwd, inv, back_up, back_dn = (jnp.asarray(t) for t in tables())
    col_t, row_t = blur_tables(rows * lax.axis_size("row"), rows, cols)
    where = lax.axis_index("row").astype(jnp.int32).reshape(1)

    low = jnp.stack([ifg_real[:, :HALF], ifg_imag[:, :HALF]])
    high = jnp.stack([ifg_real[:, rows - HALF :], ifg_imag[:, rows - HALF :]])
    above, below = neighbours(low, high, "row")
    u = centre(ifg_real, ifg_imag, rows_t, fwd, inv)
    p, g = projection(date_pairs)
    u, p, g = lax.optimization_barrier((u, p, g))
    series = ()
    for upper, halo, back in ((True, above, back_up), (False, below, back_dn)):
        q = edge(upper, ifg_real, ifg_imag, halo, u, rows_t, fwd, inv, back)
        sines = lax.all_to_all(q, "ifg", split_axis=0, concat_axis=0, tiled=True)
        series = (invert(sines.reshape(-1, cols), p, g, *series),)
    devices = lax.axis_size("ifg")
    series = lax.all_to_all(
        series[0].reshape(devices, -1, LANES), "ifg", split_axis=0, concat_axis=0, tiled=True
    )
    series, smooth, low, high = gather(series.reshape(-1, LANES), *halves(col_t), rows, cols)
    up, dn = neighbours(low, high, "row")
    return tuple(finish(where, series, smooth, up, dn, *halves(row_t)))


def solution(mesh):
    placed = (P("ifg", "row", None), P("ifg", "row", None), P())
    return jax.shard_map(
        on_device,
        mesh=mesh,
        in_specs=placed,
        out_specs=(P("ifg", "row", None), P("ifg", "row", None)),
        check_vma=False,
    )
```

```python
import math

import jax
import jax.numpy as jnp
import ml_dtypes
import numpy as np
from jax import lax
from jax.experimental import pallas as pl
from jax.experimental.pallas import tpu as pltpu
from jax.sharding import PartitionSpec as P

PATCH = 64
HALF = PATCH // 2
NDATES = 320
ITERS = 3
RADIUS = 16
SIGMA = 5.0
THRESHOLD = 0.3
BAND = 5
LANES = 128
DATE_PAD = 384
BF16 = jnp.bfloat16
F32 = jnp.float32


def bf16(x):
    return np.asarray(x, np.float32).astype(ml_dtypes.bfloat16)


def tables():
    n = np.arange(PATCH)
    angle = (n[:, None] * n[None, :] % PATCH) * (2.0 * math.pi / PATCH)
    c = bf16(np.cos(angle) / 8.0).astype(np.float64)
    s = bf16(np.sin(angle) / 8.0).astype(np.float64)
    taper = np.sin(math.pi * (n + 0.5) / PATCH) ** 2
    two = np.eye(2)
    zero = np.zeros((PATCH, PATCH))

    rows_strip = np.block([[c, s], [-s, c]])
    c2, s2 = np.kron(two, c), np.kron(two, s)
    forward = np.block([[c2, -s2], [s2, c2]])
    t2 = np.concatenate([taper, taper])
    inverse = np.block([[c2 * t2, s2 * t2], [-s2 * t2, c2 * t2]])
    ct, st = c * taper[:, None], s * taper[:, None]
    back = []
    for centre_rows, edge_rows in ((slice(0, HALF), slice(HALF, PATCH)), (slice(HALF, PATCH), slice(0, HALF))):
        c1, s1, c2, s2 = ct[centre_rows], st[centre_rows], ct[edge_rows], st[edge_rows]
        back.append(np.block([[c1, -s1, c2, -s2], [s1, c1, s2, c2]]))
    return tuple(bf16(x) for x in (rows_strip, forward, inverse, *back))


def gauss(distance):
    return np.where(np.abs(distance) <= RADIUS, np.exp(-0.5 * (distance / SIGMA) ** 2), 0.0)


def blur_tables(rows, local_rows, cols):
    i = np.arange(cols)
    by_col = gauss(i[:, None] - i[None, :])
    by_col = by_col / by_col.sum(0, keepdims=True)
    out = np.arange(rows)[:, None]
    src = np.arange(-RADIUS, rows + RADIUS)[None, :]
    by_row = gauss(src - out) * ((src >= 0) & (src < rows))
    by_row = by_row / by_row.sum(1, keepdims=True)
    blocks = [
        by_row[a : a + local_rows, a : a + local_rows + 2 * RADIUS]
        for a in range(0, rows, local_rows)
    ]
    return by_col.astype(np.float32), np.stack(blocks).astype(np.float32)


def mm(a, b):
    return jnp.dot(a, b, preferred_element_type=F32)


def spectral(y_re, y_im, fwd, inv):
    count = y_re.shape[1] // LANES
    pieces = []
    for c in range(count):
        sl = slice(c * LANES, (c + 1) * LANES)
        pieces.append(jnp.concatenate([y_re[:, sl], y_im[:, sl]], axis=1))
    f0, g0 = fwd[...], inv[...]

    def shaped(z):
        re, im = z[:, :LANES], z[:, LANES:]
        scale = lax.rsqrt(lax.rsqrt(re * re + im * im + 1.0))
        return jnp.concatenate([(re * scale).astype(BF16), (im * scale).astype(BF16)], axis=1)

    lane = lax.broadcasted_iota(jnp.int32, (y_re.shape[0], LANES), 1)

    def moved(y):
        rolled = [pltpu.roll(y[:, c * LANES : (c + 1) * LANES], HALF, axis=1) for c in range(count)]
        zero = jnp.zeros_like(rolled[0])
        before, after = [zero] + rolled, rolled + [zero]
        return [jnp.where(lane < HALF, a, b) for a, b in zip(before, after)]

    even = [
        shaped(mm(jnp.concatenate([a, b], axis=1), f0)) for a, b in zip(moved(y_re), moved(y_im))
    ]
    def back(z):
        u = mm(z, g0)
        return [pltpu.roll(u[:, :LANES], LANES - HALF, axis=1), pltpu.roll(u[:, LANES:], LANES - HALF, axis=1)]

    turned = [back(z) for z in even]
    out_re, out_im = [], []
    for c in range(count):
        u = mm(shaped(mm(pieces[c], f0)), g0)
        for out, k in ((out_re, 0), (out_im, 1)):
            other = jnp.where(lane < LANES - HALF, turned[c][k], turned[c + 1][k])
            out.append((u[:, k * LANES : (k + 1) * LANES] + other).astype(BF16))
    return jnp.concatenate(out_re, axis=1), jnp.concatenate(out_im, axis=1)


def stacked_rows(table, strips):
    y = [mm(table, x).astype(BF16) for x in strips]
    y_re = jnp.concatenate([t[:PATCH] for t in y], axis=0)
    y_im = jnp.concatenate([t[PATCH:] for t in y], axis=0)
    return y_re, y_im


def centre_kernel(re_ref, im_ref, rows_ref, fwd_ref, inv_ref, *refs):
    u_ref = refs[-1]
    n = re_ref.shape[0]
    strips = [jnp.concatenate([re_ref[i], im_ref[i]], axis=0) for i in range(n)]
    y_re, y_im = stacked_rows(rows_ref[...], strips)
    u_re, u_im = spectral(y_re, y_im, fwd_ref, inv_ref)
    for i in range(n):
        sl = slice(i * PATCH, (i + 1) * PATCH)
        u_ref[i, :PATCH] = u_re[sl]
        u_ref[i, PATCH:] = u_im[sl]


BATCH = 8


def in_hbm(x):
    return pltpu.with_memory_space_constraint(x, pltpu.HBM)


def whole(a):
    return pl.BlockSpec(a.shape, lambda i: (0,) * a.ndim)


def centre(re, im, rows_t, fwd, inv, *after):
    n, rows, cols = re.shape
    g = BATCH
    block = pl.BlockSpec((g, rows, cols), lambda i: (i, 0, 0))
    return pl.pallas_call(
        centre_kernel,
        grid=(n // g,),
        in_specs=[block, block, whole(rows_t), whole(fwd), whole(inv),
                  *(pl.BlockSpec(memory_space=pl.ANY) for _ in after)],
        out_specs=pl.BlockSpec((g, 2 * rows, cols), lambda i: (i, 0, 0)),
        out_shape=pltpu.HBM((n, 2 * rows, cols), BF16),
        compiler_params=pltpu.CompilerParams(vmem_limit_bytes=24 << 20),
        cost_estimate=pl.CostEstimate(
            flops=n * 2 * 64 * 256 * 256 * 26, bytes_accessed=n * rows * cols * 8,
            transcendentals=n * 64 * 2304,
        ),
        name="centre",
    )(*(in_hbm(x) for x in (re, im, rows_t, fwd, inv)), *after)


def pack_kernel(re_ref, im_ref, *out_refs):
    step, steps = pl.program_id(0), pl.num_programs(0)
    for part in range(2):

        @pl.when(step // (steps // 2) == part)
        def _():
            for side in range(2):
                out_ref = out_refs[2 * side + part]
                out_ref[0] = re_ref[:, side * HALF : (side + 1) * HALF]
                out_ref[1] = im_ref[:, side * HALF : (side + 1) * HALF]


def pack(re, im):
    n, rows, cols = re.shape
    g = BATCH
    steps = n // g
    block = pl.BlockSpec((g, rows, cols), lambda i: (i, 0, 0))
    early = pl.BlockSpec((2, g, HALF, cols), lambda i: (0, jnp.minimum(i, steps // 2 - 1), 0, 0))
    late = pl.BlockSpec((2, g, HALF, cols), lambda i: (0, jnp.maximum(i - steps // 2, 0), 0, 0))
    return pl.pallas_call(
        pack_kernel,
        grid=(steps,),
        in_specs=[block, block],
        out_specs=[early, late] * 2,
        out_shape=[jax.ShapeDtypeStruct((2, n // 2, HALF, cols), BF16)] * 4,
        compiler_params=pltpu.CompilerParams(vmem_limit_bytes=16 << 20),
        name="pack",
    )(in_hbm(re), in_hbm(im))


GROUP = 16


def edge_kernel(upper, re_ref, im_ref, halo_ref, u_ref, rows_ref, fwd_ref, inv_ref, back_ref, *refs):
    q_ref, keep = refs[-2:]
    g = re_ref.shape[0]
    part = pl.program_id(0) % (GROUP // g)
    strips = []
    for i in range(g):
        own = [re_ref[i], im_ref[i]]
        other = [halo_ref[0, i], halo_ref[1, i]]
        first, second = (other, own) if upper else (own, other)
        strips.append(jnp.concatenate([first[0], second[0], first[1], second[1]], axis=0))
    y_re, y_im = stacked_rows(rows_ref[...], strips)
    u_re, u_im = spectral(y_re, y_im, fwd_ref, inv_ref)
    for i in range(g):
        sl = slice(i * PATCH, (i + 1) * PATCH)
        f = mm(back_ref[...], jnp.concatenate([u_ref[i], u_re[sl], u_im[sl]], axis=0))
        re, im = f[:HALF], f[HALF:]
        q = im * lax.rsqrt(re * re + im * im + 1.0)
        for c in range(keep.shape[0]):
            keep[c, pl.ds(part * g + i, HALF, stride=GROUP), :] = q[:, c * LANES : (c + 1) * LANES]

    @pl.when(part == GROUP // g - 1)
    def _():
        for t in range(keep.shape[0]):
            block = keep[t].astype(BF16)
            q_ref[:, :, t * LANES : (t + 1) * LANES] = block.reshape(HALF, GROUP, LANES)


def edge(upper, first, re, im, halo, u, rows_t, fwd, inv, back, *done):
    n, rows, cols = re.shape
    g = BATCH
    side = 0 if upper else 1
    at = first // g
    block = pl.BlockSpec((g, HALF, cols), lambda i: (at + i, side, 0))
    operands = [re, im, halo, u, rows_t, fwd, inv, back]
    return pl.pallas_call(
        lambda *refs: edge_kernel(upper, *refs),
        grid=(halo.shape[1] // g,),
        in_specs=[block, block,
                  pl.BlockSpec((2, g, HALF, cols), lambda i: (0, i, 0, 0)),
                  pl.BlockSpec((g, 2 * rows, cols), lambda i: (at + i, 0, 0)),
                  *(whole(x) for x in operands[4:]),
                  *(pl.BlockSpec(memory_space=pl.ANY) for _ in done)],
        out_specs=pl.BlockSpec((HALF, GROUP, cols), lambda i: (0, (first + i * g) // GROUP, 0)),
        out_shape=pltpu.HBM((HALF, n, cols), BF16),
        scratch_shapes=[pltpu.VMEM((cols // LANES, HALF * GROUP, LANES), F32)],
        input_output_aliases={len(operands): 0} if done else {},
        compiler_params=pltpu.CompilerParams(vmem_limit_bytes=24 << 20),
        cost_estimate=pl.CostEstimate(
            flops=halo.shape[1] * 2 * 64 * 256 * 256 * 30,
            bytes_accessed=halo.shape[1] * rows * cols * 7,
            transcendentals=halo.shape[1] * 64 * 2304,
        ),
        name="upper" if upper else "lower",
    )(*(x if x is halo else in_hbm(x) for x in operands), *(in_hbm(x) for x in done))


def projection_kernel(pairs_ref, pairs_t_ref, p_ref, g_ref, band, factor, solved):
    nifg = pairs_ref.shape[0]
    first, second = pairs_ref[:, 0:1], pairs_ref[:, 1:2]
    def design(width, wrap):
        dates = lax.broadcasted_iota(jnp.int32, (nifg, width), 1)
        if wrap:
            dates = jnp.where(dates >= NDATES, dates - NDATES, dates)
        return (jnp.where(dates == second, 1.0, 0.0) - jnp.where(dates == first, 1.0, 0.0)).astype(BF16)

    g_ref[...] = design(2 * NDATES, True)
    single = design(DATE_PAD, False)

    row_date = lax.broadcasted_iota(jnp.int32, (NDATES, nifg), 0)
    is_first = row_date == pairs_t_ref[0:1, :]
    is_either = is_first | (row_date == pairs_t_ref[1:2, :])
    first_t = jnp.where(is_first, 1.0, 0.0).astype(BF16)
    either_t = jnp.where(is_either, 1.0, 0.0).astype(BF16)
    gap = jnp.broadcast_to(second - first, (nifg, LANES))
    degree = mm(either_t, jnp.ones((nifg, LANES), BF16)) + 1.0
    band[...] = jnp.zeros_like(band)
    band[pl.ds(0, NDATES, stride=8), :] = degree
    for j in range(1, BAND + 1):
        match = jnp.where(gap == j, 1.0, 0.0).astype(BF16)
        band[pl.ds(j, NDATES, stride=8), :] = -mm(first_t, match)

    sub = lax.broadcasted_iota(jnp.int32, (8, LANES), 0)
    flat = sub * LANES + lax.broadcasted_iota(jnp.int32, (8, LANES), 1)

    def unit(i):
        return jnp.where(flat == i, 1.0, 0.0)

    def spread(x, j):
        return jnp.broadcast_to(x[j : j + 1, :], (8, LANES))

    def down(i, carry):
        rows, rhs = list(carry[: BAND + 1]), list(carry[BAND + 1 :])
        r, x = rows[0], rhs[0]
        inv = 1.0 / spread(r, 0)
        scaled = r * inv
        at = pl.ds(pl.multiple_of(i * 8, 8), 8)
        factor[at, :] = scaled
        solved[at, :] = x * inv
        for j in range(1, BAND + 1):
            moved = jnp.where(sub <= BAND - j, pltpu.roll(r, 8 - j, axis=0), 0.0)
            rows[j] = rows[j] - (spread(r, j) * moved) * inv
            rhs[j] = rhs[j] - spread(scaled, j) * x
        ahead = i + BAND + 1
        rows = rows[1:] + [band[pl.ds(pl.multiple_of(ahead * 8, 8), 8), :]]
        rhs = rhs[1:] + [unit(ahead)]
        return tuple(rows + rhs)

    start = [band[j * 8 : (j + 1) * 8, :] for j in range(BAND + 1)]
    start += [unit(j) for j in range(BAND + 1)]
    lax.fori_loop(0, NDATES, down, tuple(start), unroll=4)

    def up(t, carry):
        i = NDATES - 1 - t
        at = pl.ds(pl.multiple_of(i * 8, 8), 8)
        l = factor[at, :]
        x = solved[at, :]
        for j in range(BAND, 0, -1):
            x = x - spread(l, j) * carry[j - 1]
        solved[at, :] = x
        return (x,) + carry[:-1]

    zero = band[pl.ds((NDATES + BAND) * 8, 8), :]
    lax.fori_loop(0, NDATES, up, (zero,) * BAND, unroll=8)

    total = jnp.zeros((NDATES, nifg), F32)
    inverse = jnp.concatenate(
        [solved[pl.ds(c, NDATES, stride=8), :] for c in range(DATE_PAD // LANES)], axis=1
    )
    rest = inverse
    for _ in range(3):
        part = rest.astype(BF16)
        rest = rest - part.astype(F32)
        total = total + lax.dot_general(
            part, single, (((1,), (1,)), ((), ())), preferred_element_type=F32
        )
    high = total.astype(BF16)
    p_ref[...] = high


def projection(date_pairs):
    nifg = date_pairs.shape[0]
    tail = (NDATES + 2 * BAND + 6) * 8
    return pl.pallas_call(
        projection_kernel,
        out_shape=(
            pltpu.HBM((NDATES, nifg), BF16),
            pltpu.HBM((nifg, 2 * NDATES), BF16),
        ),
        scratch_shapes=[
            pltpu.VMEM((tail, LANES), F32),
            pltpu.VMEM((NDATES * 8, LANES), F32),
            pltpu.VMEM((NDATES * 8, LANES), F32),
        ],
        compiler_params=pltpu.CompilerParams(vmem_limit_bytes=40 << 20),
        cost_estimate=pl.CostEstimate(
            flops=20_000_000_000, bytes_accessed=4_000_000, transcendentals=0
        ),
        name="projection",
    )(date_pairs, date_pairs.T)


def invert_kernel(d_ref, p_ref, g_ref, *refs):
    chains = range(d_ref.shape[1] // CHAIN)
    scaled = [d_ref[:, k * CHAIN : (k + 1) * CHAIN].astype(F32) * (1.0 / THRESHOLD) for k in chains]
    series = [None for k in chains]
    misfit = scaled
    for step in range(ITERS):
        if step > 0:
            parts = []
            for k in chains:
                high = series[k].astype(BF16)
                low = (series[k] - high.astype(F32)).astype(BF16)
                parts.append(jnp.concatenate([high, low], axis=0))
            misfit = [scaled[k] - mm(g_ref[...], parts[k]) for k in chains]
        change = [mm(p_ref[...], jnp.clip(misfit[k], -1.0, 1.0).astype(BF16)) for k in chains]
        series = [change[k] if step == 0 else series[k] + change[k] for k in chains]
    series = jnp.concatenate(series, axis=1) * THRESHOLD
    tiles = series.shape[1] // LANES
    place = pl.program_id(0) * tiles
    if len(refs) == 1:
        (m_ref,) = refs
        for t in range(tiles):
            m_ref[pl.ds(place + t, NDATES, stride=4), :] = series[:, t * LANES : (t + 1) * LANES]
        return
    other_ref, m_ref, keep = refs
    for t in range(tiles):
        keep[pl.ds(4 + place + t, NDATES, stride=8), :] = series[:, t * LANES : (t + 1) * LANES]

    @pl.when(pl.program_id(0) == pl.num_programs(0) - 1)
    def _():
        for t in range(4):
            keep[pl.ds(t, NDATES, stride=8), :] = other_ref[pl.ds(t, NDATES, stride=4), :]
        m_ref[...] = keep[...].astype(BF16)


WIDTH = 512
CHAIN = 512


def invert(sines, p, g, *other):
    nifg, pixels = sines.shape
    width = WIDTH
    rows = NDATES * (8 if other else 4)
    return pl.pallas_call(
        invert_kernel,
        grid=(pixels // width,),
        in_specs=[
            pl.BlockSpec((nifg, width), lambda i: (0, i)),
            whole(p), whole(g), *(whole(x) for x in other)
        ],
        out_specs=pl.BlockSpec((rows, LANES), lambda i: (0, 0)),
        out_shape=jax.ShapeDtypeStruct((rows, LANES), BF16) if other else pltpu.HBM((rows, LANES), F32),
        scratch_shapes=[pltpu.VMEM((rows, LANES), F32)] if other else [],
        compiler_params=pltpu.CompilerParams(vmem_limit_bytes=32 << 20),
        cost_estimate=pl.CostEstimate(
            flops=pixels * nifg * NDATES * 14, bytes_accessed=6_000_000, transcendentals=0
        ),
        name="invert_rest" if other else "invert",
    )(sines, in_hbm(p), in_hbm(g), *(in_hbm(x) for x in other))


def halves(table):
    high = bf16(table)
    return jnp.asarray(high), jnp.asarray(bf16(table - high.astype(np.float32)))


def split2(x):
    high = x.astype(BF16)
    return high, (x - high.astype(F32)).astype(BF16)


def dot3(a, b):
    (ah, al), (bh, bl) = a, b
    return mm(ah, bh) + (mm(ah, bl) + mm(al, bh))


def gather_kernel(got_ref, ch_ref, cl_ref, series_ref, smooth_ref, low_ref, high_ref, wide):
    dates, rows, cols = series_ref.shape
    tiles = cols // LANES
    wide[...] = got_ref[...].astype(F32)
    for d in range(dates):
        halves = []
        for h in range(2):
            halves.append(
                jnp.concatenate(
                    [
                        wide[pl.ds(d * 8 + h * tiles + c, HALF, stride=dates * 8), :]
                        for c in range(tiles)
                    ],
                    axis=1,
                )
            )
        x = jnp.concatenate(halves, axis=0)
        series_ref[d] = x
        x = x.astype(BF16)
        smooth = mm(x, ch_ref[...]) + mm(x, cl_ref[...])
        smooth_ref[d] = smooth
        low_ref[d] = smooth[:RADIUS].astype(BF16)
        high_ref[d] = smooth[rows - RADIUS :].astype(BF16)


def gather(got, col_high, col_low, rows, cols):
    dates = got.shape[0] // 8 // HALF
    block = jax.ShapeDtypeStruct((dates, rows, cols), F32)
    border = jax.ShapeDtypeStruct((dates, RADIUS, cols), BF16)
    return pl.pallas_call(
        gather_kernel,
        out_shape=(block, block, border, border),
        scratch_shapes=[pltpu.VMEM(got.shape, F32)],
        compiler_params=pltpu.CompilerParams(vmem_limit_bytes=24 << 20),
        name="gather",
    )(got, col_high, col_low)


def finish_kernel(where_ref, series_ref, smooth_ref, up_ref, dn_ref, high_ref, low_ref, corr_ref, atm_ref):
    table = (high_ref[0], low_ref[0])
    for d in range(series_ref.shape[0]):
        smooth, rest = split2(smooth_ref[d])
        x = jnp.concatenate([up_ref[d], smooth, dn_ref[d]], axis=0)
        atm = mm(table[0], x) + (mm(table[1], x) + mm(table[0][:, RADIUS:-RADIUS], rest))
        atm_ref[d] = atm
        corr_ref[d] = series_ref[d] - atm


def finish(where, series, smooth, up, dn, high, low):
    dates, rows, cols = series.shape
    g = FINISH
    block = pl.BlockSpec((g, rows, cols), lambda i, w: (i, 0, 0))
    halo = pl.BlockSpec((g, RADIUS, cols), lambda i, w: (i, 0, 0))
    table = pl.BlockSpec((1,) + high.shape[1:], lambda i, w: (w[0], 0, 0))
    return pl.pallas_call(
        finish_kernel,
        grid_spec=pltpu.PrefetchScalarGridSpec(
            num_scalar_prefetch=1,
            grid=(dates // g,),
            in_specs=[block, block, halo, halo, table, table],
            out_specs=[block, block],
        ),
        out_shape=(jax.ShapeDtypeStruct((dates, rows, cols), F32),) * 2,
        compiler_params=pltpu.CompilerParams(vmem_limit_bytes=24 << 20),
        name="finish",
    )(where, series, smooth, up, dn, high, low)


FINISH = 5


def neighbours(low_part, high_part, axis):
    count = lax.axis_size(axis)
    forward = [(i, i + 1) for i in range(count - 1)]
    backward = [(b, a) for a, b in forward]
    return lax.ppermute(high_part, axis, forward), lax.ppermute(low_part, axis, backward)


def on_device(ifg_real, ifg_imag, date_pairs):
    n, rows, cols = ifg_real.shape
    rows_t, fwd, inv, back_up, back_dn = (jnp.asarray(t) for t in tables())
    col_t, row_t = blur_tables(rows * lax.axis_size("row"), rows, cols)
    where = lax.axis_index("row").astype(jnp.int32).reshape(1)

    count = lax.axis_size("row")
    onward = [(i, i + 1) for i in range(count - 1)]
    back = [(b, a) for a, b in onward]
    packed = pack(ifg_real, ifg_imag)
    above = [lax.ppermute(part, "row", onward) for part in packed[2:]]
    below = [lax.ppermute(part, "row", back) for part in packed[:2]]
    u = centre(ifg_real, ifg_imag, rows_t, fwd, inv, packed[2])
    p, g = projection(date_pairs)
    sides = []
    for upper, parts, table in ((True, above, back_up), (False, below, back_dn)):
        q = ()
        for k, halo in enumerate(parts):
            q = (edge(upper, k * (n // 2), ifg_real, ifg_imag, halo, u, rows_t, fwd, inv, table, *q),)
        sides += q
    series = ()
    for part in sides:
        sines = lax.all_to_all(part, "ifg", split_axis=0, concat_axis=0, tiled=True)
        series = (invert(sines.reshape(-1, cols), p, g, *series),)
    devices = lax.axis_size("ifg")
    series = lax.all_to_all(
        series[0].reshape(devices, -1, LANES), "ifg", split_axis=0, concat_axis=0, tiled=True
    )
    series, smooth, low, high = gather(series.reshape(-1, LANES), *halves(col_t), rows, cols)
    up, dn = neighbours(low, high, "row")
    return tuple(finish(where, series, smooth, up, dn, *halves(row_t)))


def solution(mesh):
    placed = (P("ifg", "row", None), P("ifg", "row", None), P())
    return jax.shard_map(
        on_device,
        mesh=mesh,
        in_specs=placed,
        out_specs=(P("ifg", "row", None), P("ifg", "row", None)),
        check_vma=False,
    )
```

```python
import math

import jax
import jax.numpy as jnp
import ml_dtypes
import numpy as np
from jax import lax
from jax.experimental import pallas as pl
from jax.experimental.pallas import tpu as pltpu
from jax.sharding import PartitionSpec as P

PATCH = 64
HALF = PATCH // 2
NDATES = 320
ITERS = 3
RADIUS = 16
SIGMA = 5.0
THRESHOLD = 0.3
BAND = 5
LANES = 128
DATE_PAD = 384
BF16 = jnp.bfloat16
F32 = jnp.float32


def bf16(x):
    return np.asarray(x, np.float32).astype(ml_dtypes.bfloat16)


def tables():
    n = np.arange(PATCH)
    angle = (n[:, None] * n[None, :] % PATCH) * (2.0 * math.pi / PATCH)
    c = bf16(np.cos(angle) / 8.0).astype(np.float64)
    s = bf16(np.sin(angle) / 8.0).astype(np.float64)
    taper = np.sin(math.pi * (n + 0.5) / PATCH) ** 2
    two = np.eye(2)
    zero = np.zeros((PATCH, PATCH))

    rows_strip = np.block([[c, s], [-s, c]])
    c2, s2 = np.kron(two, c), np.kron(two, s)
    forward = np.block([[c2, -s2], [s2, c2]])
    t2 = np.concatenate([taper, taper])
    inverse = np.block([[c2 * t2, s2 * t2], [-s2 * t2, c2 * t2]])
    ct, st = c * taper[:, None], s * taper[:, None]
    back = []
    for centre_rows, edge_rows in ((slice(0, HALF), slice(HALF, PATCH)), (slice(HALF, PATCH), slice(0, HALF))):
        c1, s1, c2, s2 = ct[centre_rows], st[centre_rows], ct[edge_rows], st[edge_rows]
        back.append(np.block([[c1, -s1, c2, -s2], [s1, c1, s2, c2]]))
    return tuple(bf16(x) for x in (rows_strip, forward, inverse, *back))


def gauss(distance):
    return np.where(np.abs(distance) <= RADIUS, np.exp(-0.5 * (distance / SIGMA) ** 2), 0.0)


def blur_tables(rows, local_rows, cols):
    i = np.arange(cols)
    by_col = gauss(i[:, None] - i[None, :])
    by_col = by_col / by_col.sum(0, keepdims=True)
    out = np.arange(rows)[:, None]
    src = np.arange(-RADIUS, rows + RADIUS)[None, :]
    by_row = gauss(src - out) * ((src >= 0) & (src < rows))
    by_row = by_row / by_row.sum(1, keepdims=True)
    blocks = [
        by_row[a : a + local_rows, a : a + local_rows + 2 * RADIUS]
        for a in range(0, rows, local_rows)
    ]
    return by_col.astype(np.float32), np.stack(blocks).astype(np.float32)


def mm(a, b):
    return jnp.dot(a, b, preferred_element_type=F32)


def spectral(y_re, y_im, fwd, inv):
    count = y_re.shape[1] // LANES
    pieces = []
    for c in range(count):
        sl = slice(c * LANES, (c + 1) * LANES)
        pieces.append(jnp.concatenate([y_re[:, sl], y_im[:, sl]], axis=1))
    f0, g0 = fwd[...], inv[...]

    def shaped(z):
        re, im = z[:, :LANES], z[:, LANES:]
        scale = lax.rsqrt(lax.rsqrt(re * re + im * im + 1.0))
        return jnp.concatenate([(re * scale).astype(BF16), (im * scale).astype(BF16)], axis=1)

    lane = lax.broadcasted_iota(jnp.int32, (y_re.shape[0], LANES), 1)

    def moved(y):
        rolled = [pltpu.roll(y[:, c * LANES : (c + 1) * LANES], HALF, axis=1) for c in range(count)]
        zero = jnp.zeros_like(rolled[0])
        before, after = [zero] + rolled, rolled + [zero]
        return [jnp.where(lane < HALF, a, b) for a, b in zip(before, after)]

    even = [
        shaped(mm(jnp.concatenate([a, b], axis=1), f0)) for a, b in zip(moved(y_re), moved(y_im))
    ]
    def back(z):
        u = mm(z, g0)
        return [pltpu.roll(u[:, :LANES], LANES - HALF, axis=1), pltpu.roll(u[:, LANES:], LANES - HALF, axis=1)]

    turned = [back(z) for z in even]
    out_re, out_im = [], []
    for c in range(count):
        u = mm(shaped(mm(pieces[c], f0)), g0)
        for out, k in ((out_re, 0), (out_im, 1)):
            other = jnp.where(lane < LANES - HALF, turned[c][k], turned[c + 1][k])
            out.append((u[:, k * LANES : (k + 1) * LANES] + other).astype(BF16))
    return jnp.concatenate(out_re, axis=1), jnp.concatenate(out_im, axis=1)


def stacked_rows(table, strips):
    y = [mm(table, x).astype(BF16) for x in strips]
    y_re = jnp.concatenate([t[:PATCH] for t in y], axis=0)
    y_im = jnp.concatenate([t[PATCH:] for t in y], axis=0)
    return y_re, y_im


def centre_kernel(re_ref, im_ref, rows_ref, fwd_ref, inv_ref, u_ref):
    n = re_ref.shape[0]
    strips = [jnp.concatenate([re_ref[i], im_ref[i]], axis=0) for i in range(n)]
    y_re, y_im = stacked_rows(rows_ref[...], strips)
    u_re, u_im = spectral(y_re, y_im, fwd_ref, inv_ref)
    for i in range(n):
        sl = slice(i * PATCH, (i + 1) * PATCH)
        u_ref[i, :PATCH] = u_re[sl]
        u_ref[i, PATCH:] = u_im[sl]


BATCH = 8


def in_hbm(x):
    return pltpu.with_memory_space_constraint(x, pltpu.HBM)


def whole(a):
    return pl.BlockSpec(a.shape, lambda i: (0,) * a.ndim)


def centre(re, im, rows_t, fwd, inv):
    n, rows, cols = re.shape
    g = BATCH
    block = pl.BlockSpec((g, rows, cols), lambda i: (i, 0, 0))
    return pl.pallas_call(
        centre_kernel,
        grid=(n // g,),
        in_specs=[block, block, whole(rows_t), whole(fwd), whole(inv)],
        out_specs=pl.BlockSpec((g, 2 * rows, cols), lambda i: (i, 0, 0)),
        out_shape=pltpu.HBM((n, 2 * rows, cols), BF16),
        compiler_params=pltpu.CompilerParams(vmem_limit_bytes=24 << 20),
        cost_estimate=pl.CostEstimate(
            flops=n * 2 * 64 * 256 * 256 * 26, bytes_accessed=n * rows * cols * 8,
            transcendentals=n * 64 * 2304,
        ),
        name="centre",
    )(*(in_hbm(x) for x in (re, im, rows_t, fwd, inv)))


GROUP = 16


def edge_kernel(upper, re_ref, im_ref, halo_ref, u_ref, rows_ref, fwd_ref, inv_ref, back_ref, q_ref, keep):
    g = re_ref.shape[0]
    part = pl.program_id(0) % (GROUP // g)
    strips = []
    for i in range(g):
        own = [re_ref[i], im_ref[i]]
        other = [halo_ref[0, i], halo_ref[1, i]]
        first, second = (other, own) if upper else (own, other)
        strips.append(jnp.concatenate([first[0], second[0], first[1], second[1]], axis=0))
    y_re, y_im = stacked_rows(rows_ref[...], strips)
    u_re, u_im = spectral(y_re, y_im, fwd_ref, inv_ref)
    for i in range(g):
        sl = slice(i * PATCH, (i + 1) * PATCH)
        f = mm(back_ref[...], jnp.concatenate([u_ref[i], u_re[sl], u_im[sl]], axis=0))
        re, im = f[:HALF], f[HALF:]
        q = im * lax.rsqrt(re * re + im * im + 1.0)
        for c in range(keep.shape[0]):
            keep[c, pl.ds(part * g + i, HALF, stride=GROUP), :] = q[:, c * LANES : (c + 1) * LANES]

    @pl.when(part == GROUP // g - 1)
    def _():
        for t in range(keep.shape[0]):
            block = keep[t].astype(BF16)
            q_ref[:, :, t * LANES : (t + 1) * LANES] = block.reshape(HALF, GROUP, LANES)


def edge(upper, re, im, halo, u, rows_t, fwd, inv, back):
    n, rows, cols = re.shape
    g = BATCH
    side = 0 if upper else 1
    block = pl.BlockSpec((g, HALF, cols), lambda i: (i, side, 0))
    return pl.pallas_call(
        lambda *refs: edge_kernel(upper, *refs),
        grid=(n // g,),
        in_specs=[block, block,
                  pl.BlockSpec((2, g, HALF, cols), lambda i: (0, i, 0, 0)),
                  pl.BlockSpec((g, 2 * rows, cols), lambda i: (i, 0, 0)),
                  whole(rows_t), whole(fwd), whole(inv), whole(back)],
        out_specs=pl.BlockSpec((HALF, GROUP, cols), lambda i: (0, i // (GROUP // g), 0)),
        out_shape=pltpu.HBM((HALF, n, cols), BF16),
        scratch_shapes=[pltpu.VMEM((cols // LANES, HALF * GROUP, LANES), F32)],
        compiler_params=pltpu.CompilerParams(vmem_limit_bytes=24 << 20),
        cost_estimate=pl.CostEstimate(
            flops=n * 2 * 64 * 256 * 256 * 30, bytes_accessed=n * rows * cols * 7,
            transcendentals=n * 64 * 2304,
        ),
        name="upper" if upper else "lower",
    )(in_hbm(re), in_hbm(im), halo, *(in_hbm(x) for x in (u, rows_t, fwd, inv, back)))


def projection_kernel(pairs_ref, pairs_t_ref, p_ref, g_ref, band, factor, solved):
    nifg = pairs_ref.shape[0]
    first, second = pairs_ref[:, 0:1], pairs_ref[:, 1:2]
    def design(width, wrap):
        dates = lax.broadcasted_iota(jnp.int32, (nifg, width), 1)
        if wrap:
            dates = jnp.where(dates >= NDATES, dates - NDATES, dates)
        return (jnp.where(dates == second, 1.0, 0.0) - jnp.where(dates == first, 1.0, 0.0)).astype(BF16)

    g_ref[...] = design(2 * NDATES, True)
    single = design(DATE_PAD, False)

    row_date = lax.broadcasted_iota(jnp.int32, (NDATES, nifg), 0)
    is_first = row_date == pairs_t_ref[0:1, :]
    is_either = is_first | (row_date == pairs_t_ref[1:2, :])
    first_t = jnp.where(is_first, 1.0, 0.0).astype(BF16)
    either_t = jnp.where(is_either, 1.0, 0.0).astype(BF16)
    gap = jnp.broadcast_to(second - first, (nifg, LANES))
    degree = mm(either_t, jnp.ones((nifg, LANES), BF16)) + 1.0
    band[...] = jnp.zeros_like(band)
    band[pl.ds(0, NDATES, stride=8), :] = degree
    for j in range(1, BAND + 1):
        match = jnp.where(gap == j, 1.0, 0.0).astype(BF16)
        band[pl.ds(j, NDATES, stride=8), :] = -mm(first_t, match)

    sub = lax.broadcasted_iota(jnp.int32, (8, LANES), 0)
    flat = sub * LANES + lax.broadcasted_iota(jnp.int32, (8, LANES), 1)

    def unit(i):
        return jnp.where(flat == i, 1.0, 0.0)

    def spread(x, j):
        return jnp.broadcast_to(x[j : j + 1, :], (8, LANES))

    def down(i, carry):
        rows, rhs = list(carry[: BAND + 1]), list(carry[BAND + 1 :])
        r, x = rows[0], rhs[0]
        inv = 1.0 / spread(r, 0)
        scaled = r * inv
        at = pl.ds(pl.multiple_of(i * 8, 8), 8)
        factor[at, :] = scaled
        solved[at, :] = x * inv
        for j in range(1, BAND + 1):
            moved = jnp.where(sub <= BAND - j, pltpu.roll(r, 8 - j, axis=0), 0.0)
            rows[j] = rows[j] - (spread(r, j) * moved) * inv
            rhs[j] = rhs[j] - spread(scaled, j) * x
        ahead = i + BAND + 1
        rows = rows[1:] + [band[pl.ds(pl.multiple_of(ahead * 8, 8), 8), :]]
        rhs = rhs[1:] + [unit(ahead)]
        return tuple(rows + rhs)

    start = [band[j * 8 : (j + 1) * 8, :] for j in range(BAND + 1)]
    start += [unit(j) for j in range(BAND + 1)]
    lax.fori_loop(0, NDATES, down, tuple(start), unroll=8)

    def up(t, carry):
        i = NDATES - 1 - t
        at = pl.ds(pl.multiple_of(i * 8, 8), 8)
        l = factor[at, :]
        x = solved[at, :]
        for j in range(BAND, 0, -1):
            x = x - spread(l, j) * carry[j - 1]
        solved[at, :] = x
        return (x,) + carry[:-1]

    zero = band[pl.ds((NDATES + BAND) * 8, 8), :]
    lax.fori_loop(0, NDATES, up, (zero,) * BAND, unroll=16)

    total = jnp.zeros((NDATES, nifg), F32)
    inverse = jnp.concatenate(
        [solved[pl.ds(c, NDATES, stride=8), :] for c in range(DATE_PAD // LANES)], axis=1
    )
    rest = inverse
    for _ in range(3):
        part = rest.astype(BF16)
        rest = rest - part.astype(F32)
        total = total + lax.dot_general(
            part, single, (((1,), (1,)), ((), ())), preferred_element_type=F32
        )
    high = total.astype(BF16)
    p_ref[...] = high


def projection(date_pairs):
    nifg = date_pairs.shape[0]
    tail = (NDATES + 2 * BAND + 6) * 8
    return pl.pallas_call(
        projection_kernel,
        out_shape=(
            pltpu.HBM((NDATES, nifg), BF16),
            pltpu.HBM((nifg, 2 * NDATES), BF16),
        ),
        scratch_shapes=[
            pltpu.VMEM((tail, LANES), F32),
            pltpu.VMEM((NDATES * 8, LANES), F32),
            pltpu.VMEM((NDATES * 8, LANES), F32),
        ],
        compiler_params=pltpu.CompilerParams(vmem_limit_bytes=40 << 20),
        cost_estimate=pl.CostEstimate(
            flops=20_000_000_000, bytes_accessed=4_000_000, transcendentals=0
        ),
        name="projection",
    )(date_pairs, date_pairs.T)


def invert_kernel(d_ref, p_ref, g_ref, *refs):
    chains = range(d_ref.shape[1] // CHAIN)
    scaled = [d_ref[:, k * CHAIN : (k + 1) * CHAIN].astype(F32) * (1.0 / THRESHOLD) for k in chains]
    series = [None for k in chains]
    misfit = scaled
    for step in range(ITERS):
        if step > 0:
            parts = []
            for k in chains:
                high = series[k].astype(BF16)
                low = (series[k] - high.astype(F32)).astype(BF16)
                parts.append(jnp.concatenate([high, low], axis=0))
            misfit = [scaled[k] - mm(g_ref[...], parts[k]) for k in chains]
        change = [mm(p_ref[...], jnp.clip(misfit[k], -1.0, 1.0).astype(BF16)) for k in chains]
        series = [change[k] if step == 0 else series[k] + change[k] for k in chains]
    series = jnp.concatenate(series, axis=1) * THRESHOLD
    tiles = series.shape[1] // LANES
    place = pl.program_id(0) * tiles
    if len(refs) == 1:
        (m_ref,) = refs
        for t in range(tiles):
            m_ref[pl.ds(place + t, NDATES, stride=4), :] = series[:, t * LANES : (t + 1) * LANES]
        return
    other_ref, m_ref, keep = refs
    for t in range(tiles):
        keep[pl.ds(4 + place + t, NDATES, stride=8), :] = series[:, t * LANES : (t + 1) * LANES]

    @pl.when(pl.program_id(0) == pl.num_programs(0) - 1)
    def _():
        for t in range(4):
            keep[pl.ds(t, NDATES, stride=8), :] = other_ref[pl.ds(t, NDATES, stride=4), :]
        m_ref[...] = keep[...].astype(BF16)


WIDTH = 512
CHAIN = 512


def invert(sines, p, g, *other):
    nifg, pixels = sines.shape
    width = WIDTH
    rows = NDATES * (8 if other else 4)
    return pl.pallas_call(
        invert_kernel,
        grid=(pixels // width,),
        in_specs=[
            pl.BlockSpec((nifg, width), lambda i: (0, i)),
            whole(p), whole(g), *(whole(x) for x in other)
        ],
        out_specs=pl.BlockSpec((rows, LANES), lambda i: (0, 0)),
        out_shape=jax.ShapeDtypeStruct((rows, LANES), BF16) if other else pltpu.HBM((rows, LANES), F32),
        scratch_shapes=[pltpu.VMEM((rows, LANES), F32)] if other else [],
        compiler_params=pltpu.CompilerParams(vmem_limit_bytes=32 << 20),
        cost_estimate=pl.CostEstimate(
            flops=pixels * nifg * NDATES * 14, bytes_accessed=6_000_000, transcendentals=0
        ),
        name="invert_rest" if other else "invert",
    )(sines, in_hbm(p), in_hbm(g), *(in_hbm(x) for x in other))


def halves(table):
    high = bf16(table)
    return jnp.asarray(high), jnp.asarray(bf16(table - high.astype(np.float32)))


def split2(x):
    high = x.astype(BF16)
    return high, (x - high.astype(F32)).astype(BF16)


def dot3(a, b):
    (ah, al), (bh, bl) = a, b
    return mm(ah, bh) + (mm(ah, bl) + mm(al, bh))


def gather_kernel(got_ref, ch_ref, cl_ref, series_ref, smooth_ref, low_ref, high_ref, wide):
    dates, rows, cols = series_ref.shape
    tiles = cols // LANES
    wide[...] = got_ref[...].astype(F32)
    for d in range(dates):
        halves = []
        for h in range(2):
            halves.append(
                jnp.concatenate(
                    [
                        wide[pl.ds(d * 8 + h * tiles + c, HALF, stride=dates * 8), :]
                        for c in range(tiles)
                    ],
                    axis=1,
                )
            )
        x = jnp.concatenate(halves, axis=0)
        series_ref[d] = x
        x = x.astype(BF16)
        smooth = mm(x, ch_ref[...]) + mm(x, cl_ref[...])
        smooth_ref[d] = smooth
        low_ref[d] = smooth[:RADIUS].astype(BF16)
        high_ref[d] = smooth[rows - RADIUS :].astype(BF16)


def gather(got, col_high, col_low, rows, cols):
    dates = got.shape[0] // 8 // HALF
    block = jax.ShapeDtypeStruct((dates, rows, cols), F32)
    border = jax.ShapeDtypeStruct((dates, RADIUS, cols), BF16)
    return pl.pallas_call(
        gather_kernel,
        out_shape=(block, block, border, border),
        scratch_shapes=[pltpu.VMEM(got.shape, F32)],
        compiler_params=pltpu.CompilerParams(vmem_limit_bytes=24 << 20),
        name="gather",
    )(got, col_high, col_low)


def finish_kernel(where_ref, series_ref, smooth_ref, up_ref, dn_ref, high_ref, low_ref, corr_ref, atm_ref):
    table = (high_ref[0], low_ref[0])
    for d in range(series_ref.shape[0]):
        smooth, rest = split2(smooth_ref[d])
        x = jnp.concatenate([up_ref[d], smooth, dn_ref[d]], axis=0)
        atm = mm(table[0], x) + (mm(table[1], x) + mm(table[0][:, RADIUS:-RADIUS], rest))
        atm_ref[d] = atm
        corr_ref[d] = series_ref[d] - atm


def finish(where, series, smooth, up, dn, high, low):
    dates, rows, cols = series.shape
    g = FINISH
    block = pl.BlockSpec((g, rows, cols), lambda i, w: (i, 0, 0))
    halo = pl.BlockSpec((g, RADIUS, cols), lambda i, w: (i, 0, 0))
    table = pl.BlockSpec((1,) + high.shape[1:], lambda i, w: (w[0], 0, 0))
    return pl.pallas_call(
        finish_kernel,
        grid_spec=pltpu.PrefetchScalarGridSpec(
            num_scalar_prefetch=1,
            grid=(dates // g,),
            in_specs=[block, block, halo, halo, table, table],
            out_specs=[block, block],
        ),
        out_shape=(jax.ShapeDtypeStruct((dates, rows, cols), F32),) * 2,
        compiler_params=pltpu.CompilerParams(vmem_limit_bytes=24 << 20),
        name="finish",
    )(where, series, smooth, up, dn, high, low)


FINISH = 5


def neighbours(low_part, high_part, axis):
    count = lax.axis_size(axis)
    forward = [(i, i + 1) for i in range(count - 1)]
    backward = [(b, a) for a, b in forward]
    return lax.ppermute(high_part, axis, forward), lax.ppermute(low_part, axis, backward)


def on_device(ifg_real, ifg_imag, date_pairs):
    n, rows, cols = ifg_real.shape
    rows_t, fwd, inv, back_up, back_dn = (jnp.asarray(t) for t in tables())
    col_t, row_t = blur_tables(rows * lax.axis_size("row"), rows, cols)
    where = lax.axis_index("row").astype(jnp.int32).reshape(1)

    low = jnp.stack([ifg_real[:, :HALF], ifg_imag[:, :HALF]])
    high = jnp.stack([ifg_real[:, rows - HALF :], ifg_imag[:, rows - HALF :]])
    above, below = neighbours(low, high, "row")
    u = centre(ifg_real, ifg_imag, rows_t, fwd, inv)
    p, g = projection(date_pairs)
    u, p, g = lax.optimization_barrier((u, p, g))
    series = ()
    for upper, halo, back in ((True, above, back_up), (False, below, back_dn)):
        q = edge(upper, ifg_real, ifg_imag, halo, u, rows_t, fwd, inv, back)
        sines = lax.all_to_all(q, "ifg", split_axis=0, concat_axis=0, tiled=True)
        series = (invert(sines.reshape(-1, cols), p, g, *series),)
    devices = lax.axis_size("ifg")
    series = lax.all_to_all(
        series[0].reshape(devices, -1, LANES), "ifg", split_axis=0, concat_axis=0, tiled=True
    )
    series, smooth, low, high = gather(series.reshape(-1, LANES), *halves(col_t), rows, cols)
    up, dn = neighbours(low, high, "row")
    return tuple(finish(where, series, smooth, up, dn, *halves(row_t)))


def solution(mesh):
    placed = (P("ifg", "row", None), P("ifg", "row", None), P())
    return jax.shard_map(
        on_device,
        mesh=mesh,
        in_specs=placed,
        out_specs=(P("ifg", "row", None), P("ifg", "row", None)),
        check_vma=False,
    )
```
